256 devices in a mesh: sector: 64 (over y_lo, z, x), level: 4 (over y_hi, core).
Axes of the slice: x: 4, y: 4 (y_hi: 2, y_lo: 2; y = y_hi * 2 + y_lo), z: 8, core: 2. Of those that a mesh axis runs over, the one named last changes fastest.
Arguments:
- nodes: bfloat16 [4, 1536, 48, 768], P(None, 'sector', 'level'), may hold values from -6 to 6
- level_mask: int32 [48], replicated, may hold values from 0 to 1, as said below
- source_weight: bfloat16 [768, 768], replicated, may hold values from -0.21875 to 0.21875
- target_weight: bfloat16 [768, 768], replicated, may hold values from -0.21875 to 0.21875
- direction_bias: float32 [4, 768], replicated, may hold values from -6 to 6
- node_weight: bfloat16 [768, 768], replicated, may hold values from -0.21875 to 0.21875
- query_key: bfloat16 [2, 768, 768], replicated, may hold values from -1 to 1
- value_weight: bfloat16 [768, 768], replicated, may hold values from -0.21875 to 0.21875
- output_weight: bfloat16 [768, 768], replicated, may hold values from -0.21875 to 0.21875
Outputs:
- mixed: bfloat16 [4, 1536, 48, 768], P(None, 'sector', 'level')
The draws below stay inside these ranges and needn't reach their ends.
Inputs may be any that keep to these rules, and one draw needn't show every extreme that they name: `level_mask`: exactly 37 entries are 1, the rest 0.
All inputs are finite; a program needn't handle non-finite values.
Results may differ from the reference program's by a relative error of at most 0.0065.
Values may be sent and summed in bfloat16 or wider, within the bound.
No kernel may reach another device: no remote copies, remote signals or barrier semaphores. Data moves between devices by JAX's collectives and lax.ppermute only.
A program may use at most 128 MiB of HBM per device.

```python
import jax
import jax.numpy as jnp
from jax import lax

D = 768
HEAD = 64
HEADS = 12
LAT = 4
LEV = 48
VALID = 37
LON = 1536


def draw_nodes(key, part):
    key = jax.random.fold_in(key, 11)
    first = jax.random.fold_in(key, 0)
    drawn = jax.random.truncated_normal(first, -6.0, 6.0, (LAT, LON, LEV, D), jnp.float32)
    return drawn.astype(jnp.bfloat16)


def draw_level_mask(key, part):
    key = jax.random.fold_in(key, 12)
    order = jax.random.permutation(key, LEV)
    return (order < VALID).astype(jnp.int32)


def draw_query_key(key, part):
    key = jax.random.fold_in(key, 13)
    first, second = jax.random.split(key, 2)
    query_part = jax.random.truncated_normal(first, -6.0, 6.0, (D, D), jnp.float32) * D ** (-0.5)
    fresh = jax.random.truncated_normal(second, -6.0, 6.0, (D, D), jnp.float32) * D ** (-0.5)
    key_part = fresh
    return jnp.stack([query_part, key_part]).astype(jnp.bfloat16)


def gaussian(stream_key, shape, width, most, kind=jnp.bfloat16):
    values = jax.random.normal(stream_key, shape, jnp.float32) * width
    return jnp.minimum(jnp.maximum(values, -most), most).astype(kind)


def setup_inputs(seed: int = 0) -> dict:
    splits = jax.random.split(jax.random.key(seed), 10)
    return {
        "nodes": draw_nodes(jax.random.fold_in(splits[9], 71), 0),
        "level_mask": draw_level_mask(jax.random.fold_in(splits[9], 71), 0),
        "source_weight": gaussian(splits[2], (D, D), D ** -0.5, 0.21875),
        "target_weight": gaussian(splits[3], (D, D), D ** -0.5, 0.21875),
        "direction_bias": gaussian(splits[4], (4, D), 1.0, 6.0, jnp.float32),
        "node_weight": gaussian(splits[5], (D, D), D ** -0.5, 0.21875),
        "query_key": draw_query_key(jax.random.fold_in(splits[9], 71), 0),
        "value_weight": gaussian(splits[7], (D, D), D ** -0.5, 0.21875),
        "output_weight": gaussian(splits[8], (D, D), D ** -0.5, 0.21875),
    }


epsilon = 1e-06
masked_score = -1e+30

def normalize(inputs):
    widened = inputs.astype(jnp.float32)
    return widened * lax.rsqrt(lax.optimization_barrier(jnp.mean(widened * widened, axis=-1, keepdims=True)) + epsilon)

def project(inputs, weight):
    flattened = inputs.reshape(-1, inputs.shape[-1])
    product = jnp.dot(flattened, weight, preferred_element_type=jnp.float32)
    return product.reshape(inputs.shape[:-1] + (weight.shape[1],))

def attend(column_nodes, level_valid, query_key, value_weight, output_weight):
    normed = normalize(column_nodes).astype(jnp.bfloat16)
    head_shape = column_nodes.shape[:-1] + (HEADS, HEAD)
    queries = project(normed, query_key[0]).astype(jnp.bfloat16).reshape(head_shape)
    keys_all = project(normed, query_key[1]).astype(jnp.bfloat16).reshape(head_shape)
    values_all = project(normed, value_weight).astype(jnp.bfloat16).reshape(head_shape)
    scores = jnp.einsum('cqhd,ckhd->cqhk', queries.astype(jnp.float32), keys_all.astype(jnp.float32)) * HEAD ** (-0.5)
    scores = jnp.where(level_valid, scores, masked_score)
    running_max = lax.optimization_barrier(jnp.max(scores, axis=-1, keepdims=True))
    weights = jnp.where(level_valid, jnp.exp(scores - running_max), 0.0)
    denominator = lax.optimization_barrier(jnp.sum(weights, axis=-1))
    rounded = lax.optimization_barrier(weights.astype(jnp.bfloat16))
    numerator = jnp.einsum('cqhk,ckhd->cqhd', rounded.astype(jnp.float32), values_all.astype(jnp.float32))
    attended = (numerator / denominator[..., None]).astype(jnp.bfloat16).reshape(column_nodes.shape)
    return (column_nodes.astype(jnp.float32) + project(attended, output_weight)).astype(jnp.bfloat16)

def reference(nodes, level_mask, source_weight, target_weight, direction_bias, node_weight, query_key, value_weight, output_weight):
    level_valid = level_mask > 0
    normed = normalize(nodes).astype(jnp.bfloat16)
    source = project(normed, source_weight).astype(jnp.bfloat16)
    padded = jnp.pad(source, ((1, 1), (0, 0), (0, 0), (0, 0)))

    def one_row(row_index):
        row_nodes = lax.dynamic_index_in_dim(nodes, row_index, 0, keepdims=False)
        row_normed = lax.dynamic_index_in_dim(normed, row_index, 0, keepdims=False)
        target = project(row_normed, target_weight)
        row_source = lax.dynamic_index_in_dim(source, row_index, 0, keepdims=False)
        east_side = jnp.roll(row_source, -1, axis=0)
        west_side = jnp.roll(row_source, 1, axis=0)
        north_side = lax.dynamic_index_in_dim(padded, row_index, 0, keepdims=False)
        south_side = lax.dynamic_index_in_dim(padded, row_index + 2, 0, keepdims=False)
        message_sum = jax.nn.silu(target + east_side + direction_bias[0]) + jax.nn.silu(target + west_side + direction_bias[1])
        message_sum = message_sum + jnp.where(row_index >= 1, jax.nn.silu(target + north_side + direction_bias[2]), 0.0)
        message_sum = message_sum + jnp.where(row_index <= LAT - 2, jax.nn.silu(target + south_side + direction_bias[3]), 0.0)
        summed = message_sum.astype(jnp.bfloat16)
        updated = (row_nodes.astype(jnp.float32) + project(summed, node_weight)).astype(jnp.bfloat16)
        return attend(updated, level_valid, query_key, value_weight, output_weight)
    return lax.map(one_row, jnp.arange(LAT, dtype=jnp.int32))
```

```python
import functools

import jax
import jax.numpy as jnp
import numpy as np
from jax import lax
from jax.experimental import pallas as pl
from jax.experimental.pallas import tpu as pltpu
from jax.sharding import PartitionSpec as P

HEAD = 64
EPSILON = 1e-06
MASKED = -1e30
GROUP = 8
F32, BF16 = jnp.float32, jnp.bfloat16
WHOLE = pl.BlockSpec(memory_space=pltpu.VMEM)
SCALARS = pl.BlockSpec(memory_space=pltpu.SMEM)


def params(mib=24):
    return pltpu.CompilerParams(vmem_limit_bytes=mib << 20)


def normalize(x):
    return x * lax.rsqrt(jnp.mean(x * x, axis=-1, keepdims=True) + EPSILON)


def matmul(x, weight):
    return jnp.dot(x, weight, preferred_element_type=F32)


def block_of(ref, row, block, levels):
    lon = ref.shape[-2] // levels
    x = ref[row].astype(F32).reshape(levels, lon, ref.shape[-1])
    x = x[:, GROUP * block : GROUP * (block + 1)]
    return x.reshape(levels * GROUP, ref.shape[-1])


def source_kernel(nodes_ref, weight_ref, normed_ref, source_ref):
    normed = normalize(nodes_ref[0].astype(F32)).astype(BF16)
    normed_ref[0] = normed
    source_ref[0] = (matmul(normed, weight_ref[...]) * 0.5).astype(BF16)


def sources(nodes, weight):
    rows, width = nodes.shape[1:]
    block = pl.BlockSpec((1, rows, width), lambda i: (i, 0, 0))
    like = jax.ShapeDtypeStruct(nodes.shape, BF16)
    return pl.pallas_call(
        source_kernel,
        grid=(nodes.shape[0],),
        in_specs=[block, WHOLE],
        out_specs=[block, block],
        out_shape=[like, like],
        compiler_params=params(),
        cost_estimate=pl.CostEstimate(
            flops=2 * nodes.size * width, bytes_accessed=8 * nodes.size, transcendentals=0
        ),
    )(nodes, weight)


def message_kernel(blocks, levels, order, normed_ref, source_ref, nodes_ref, target_w, node_w, bias_ref, *rest):
    lon = normed_ref.shape[1] // levels
    edges = 0 in blocks or lon // GROUP - 1 in blocks
    if edges:
        west_ref, east_ref = rest[:2]
        rest = rest[2:]
    out_ref, target_ref, sum_ref = rest
    last = normed_ref.shape[0] - 1
    width = normed_ref.shape[-1]
    size = levels * GROUP
    pieces = [(i, b) for b in blocks for i in range(2)]
    x = [block_of(normed_ref, order[i], b, levels).astype(BF16) for i, b in pieces]
    target_ref[...] = matmul(jnp.concatenate(x, axis=0), target_w[...]) * 0.5
    step = 128
    for n, (i, b) in enumerate(pieces):
        row = order[i]
        north, south = jnp.maximum(row - 1, 0), jnp.minimum(row + 1, last)
        has_north = jnp.where(row >= 1, 1.0, 0.0)
        has_south = jnp.where(row <= last - 1, 1.0, 0.0)
        if edges:
            west_edge = west_ref[row].astype(F32)
            east_edge = east_ref[row].astype(F32)
        for pair in range(levels // 2):
            for lane in range(0, width, step):
                cols = slice(lane, lane + step)
                rows = slice(2 * lon * pair, 2 * lon * (pair + 1))

                def take(x):
                    x = x.reshape(2, lon, step)[:, GROUP * b : GROUP * (b + 1)]
                    return x.reshape(2 * GROUP, step)

                middle = source_ref[row, rows, cols].astype(F32)
                east = take(pltpu.roll(middle, 2 * lon - 1, 0))
                west = take(pltpu.roll(middle, 1, 0))
                if edges and b == 0:
                    at = lax.broadcasted_iota(jnp.int32, (GROUP, step), 0) == 0
                    west = jnp.concatenate(
                        [
                            jnp.where(at, west_edge[2 * pair + k : 2 * pair + k + 1, cols], west[GROUP * k : GROUP * (k + 1)])
                            for k in range(2)
                        ],
                        axis=0,
                    )
                if edges and GROUP * (b + 1) == lon:
                    at = lax.broadcasted_iota(jnp.int32, (GROUP, step), 0) == GROUP - 1
                    east = jnp.concatenate(
                        [
                            jnp.where(at, east_edge[2 * pair + k : 2 * pair + k + 1, cols], east[GROUP * k : GROUP * (k + 1)])
                            for k in range(2)
                        ],
                        axis=0,
                    )
                target = target_ref[slice(n * size + 16 * pair, n * size + 16 * (pair + 1)), cols]

                def halved_silu(other, k):
                    half = target + other + bias_ref[k : k + 1, cols] * 0.5
                    return half + half * jnp.tanh(half)

                total = halved_silu(east, 0) + halved_silu(west, 1)
                other = take(source_ref[north, rows, cols].astype(F32))
                total = total + halved_silu(other, 2) * has_north
                other = take(source_ref[south, rows, cols].astype(F32))
                total = total + halved_silu(other, 3) * has_south
                sum_ref[n * size + 16 * pair : n * size + 16 * (pair + 1), cols] = total.astype(BF16)
    update = matmul(sum_ref[...], node_w[...])
    for n, (i, b) in enumerate(pieces):
        own = block_of(nodes_ref, order[i], b, levels)
        out_ref[n // 2, n % 2] = (own + update[n * size : (n + 1) * size]).astype(BF16)


def messages(blocks, levels, order, normed, source, nodes, target_w, node_w, bias, edges=()):
    size = levels * GROUP
    width = nodes.shape[-1]
    rows = 2 * len(blocks) * size
    args = (order, normed, source, nodes, target_w, node_w, bias, *edges)
    return pl.pallas_call(
        functools.partial(message_kernel, blocks, levels),
        in_specs=[SCALARS] + [WHOLE] * (len(args) - 1),
        out_specs=WHOLE,
        out_shape=jax.ShapeDtypeStruct((len(blocks), 2, size, width), BF16),
        scratch_shapes=[pltpu.VMEM((rows, width), F32), pltpu.VMEM((rows, width), BF16)],
        compiler_params=params(),
        cost_estimate=pl.CostEstimate(
            flops=4 * rows * width * width, bytes_accessed=16 * rows * width, transcendentals=4 * rows * width
        ),
    )(*args)


def attention_kernel(
    block, own_ref, opposite_ref, sibling_ref, across_ref, bias_ref, gather_ref, scatter_ref,
    query_key, value_w, output_w, out_own, out_opposite, out_sibling, q_ref, k_ref, v_ref, att_ref,
):
    size, width = across_ref.shape
    x = jnp.concatenate([own_ref[block, 0], opposite_ref[0, 0], sibling_ref[block], across_ref[...]], axis=0)
    normed = normalize(x.astype(F32)).astype(BF16)
    normed = matmul(gather_ref[...], normed).astype(BF16)
    q_ref[...] = (matmul(normed, query_key[0]) * HEAD**-0.5).astype(BF16)
    k_ref[...] = matmul(normed, query_key[1]).astype(BF16)
    v_ref[...] = matmul(normed, value_w[...]).astype(BF16)
    levels = 4 * size // GROUP
    pair = 2 * HEAD
    low = lax.broadcasted_iota(jnp.int32, (levels, pair), 1) < HEAD
    pad = jnp.zeros((pair - 2 * levels, pair), BF16)
    bias = bias_ref[...]
    for column in range(GROUP):
        rows = slice(levels * column, levels * (column + 1))
        for lane in range(0, width, pair):
            cols = slice(lane, lane + pair)
            query, key, value = q_ref[rows, cols], k_ref[rows, cols], v_ref[rows, cols]
            zero = jnp.zeros_like(query)
            both = jnp.concatenate([jnp.where(low, query, zero), jnp.where(low, zero, query), pad], axis=0)
            scores = lax.dot_general(key, both, (((1,), (1,)), ((), ())), preferred_element_type=F32)
            scores = scores + bias
            weights = jnp.exp(scores - jnp.max(scores, axis=0, keepdims=True))
            weights = weights * (1.0 / jnp.sum(weights, axis=0, keepdims=True))
            mixed = lax.dot_general(
                weights.astype(BF16), value, (((0,), (0,)), ((), ())), preferred_element_type=F32
            )
            att_ref[rows, cols] = jnp.where(low, mixed[:levels], mixed[levels : 2 * levels]).astype(BF16)
    attended = matmul(scatter_ref[...], att_ref[...]).astype(BF16)
    out = (x.astype(F32) + matmul(attended, output_w[...])).astype(BF16)
    out_own[...] = out[:size]
    out_opposite[...] = out[size : 2 * size]
    out_sibling[0] = out[2 * size : 3 * size]
    out_sibling[1] = out[3 * size :]


def attention(block, *args):
    size, width = args[3].shape
    rows = 4 * size
    piece = jax.ShapeDtypeStruct((size, width), BF16)
    return pl.pallas_call(
        functools.partial(attention_kernel, block),
        in_specs=[WHOLE] * len(args),
        out_specs=[WHOLE] * 3,
        out_shape=[piece, piece, jax.ShapeDtypeStruct((2, size, width), BF16)],
        scratch_shapes=[pltpu.VMEM((rows, width), BF16)] * 4,
        compiler_params=params(),
        cost_estimate=pl.CostEstimate(
            flops=14 * rows * width * width, bytes_accessed=16 * rows * width, transcendentals=rows * rows
        ),
    )(*args)


def finish_kernel(blocks, levels, place, *refs):
    out_ref = refs[-1]
    own, siblings, opposites = (refs[blocks * k : blocks * (k + 1)] for k in range(3))
    width = out_ref.shape[-1]
    lon = GROUP * blocks

    def write(pieces):
        for pair in range(levels // 2):
            rows = slice(2 * GROUP * pair, 2 * GROUP * (pair + 1))
            parts = [p[rows].astype(F32).reshape(2, GROUP, width) for p in pieces]
            whole = jnp.concatenate(parts, axis=1).reshape(2 * lon, width)
            out_ref[0, 2 * lon * pair : 2 * lon * (pair + 1)] = whole.astype(BF16)

    @pl.when(pl.program_id(0) == 0)
    def _():
        write(own)

    @pl.when(pl.program_id(0) == 1)
    def _():
        write([s.at[0] for s in siblings])

    @pl.when(pl.program_id(0) == 2)
    def _():
        write([s.at[0] for s in opposites])

    @pl.when(pl.program_id(0) == 3)
    def _():
        write([s.at[1] for s in opposites])


def finish(levels, place, own, siblings, opposites):
    blocks = len(own)
    width = own[0].shape[-1]
    rows = levels * GROUP * blocks
    args = (*own, *siblings, *opposites)
    return pl.pallas_call(
        functools.partial(finish_kernel, blocks, levels),
        grid_spec=pltpu.PrefetchScalarGridSpec(
            num_scalar_prefetch=1,
            grid=(4,),
            in_specs=[WHOLE] * len(args),
            out_specs=pl.BlockSpec((1, rows, width), lambda i, place: (i ^ place[0], 0, 0)),
        ),
        out_shape=jax.ShapeDtypeStruct((4, rows, width), BF16),
        compiler_params=params(),
        cost_estimate=pl.CostEstimate(flops=0, bytes_accessed=16 * rows * width, transcendentals=0),
    )(place, *args)


def per_device(
    nodes, level_mask, source_weight, target_weight, direction_bias, node_weight, query_key, value_weight, output_weight
):
    lat, lon, levels, width = nodes.shape
    blocks = lon // GROUP
    rows = levels * lon
    here = lax.axis_index("level")
    opposite = [(i, i ^ 2) for i in range(4)]
    sibling = [(i, i ^ 1) for i in range(4)]
    ring = lax.axis_size("sector")
    up = [(i, (i + 1) % ring) for i in range(ring)]
    down = [(j, i) for i, j in up]

    nodes = jnp.transpose(nodes, (0, 2, 1, 3)).reshape(lat, rows, width)
    own_rows = jnp.stack([here, here ^ 1]).astype(jnp.int32)
    far_rows = own_rows ^ 2
    kept = jnp.where(level_mask > 0, 0.0, MASKED).astype(F32).reshape(4, levels)
    kept = jnp.concatenate([lax.dynamic_slice(kept, (here ^ k, 0), (1, levels)) for k in (0, 2, 1, 3)], axis=0)
    bias = jnp.broadcast_to(kept.reshape(4 * levels, 1), (4 * levels, 2 * HEAD))
    total = 4 * levels * GROUP
    gather = np.zeros((total, total), np.float32)
    at = np.arange(total)
    gather[at, GROUP * (at % (4 * levels)) + at // (4 * levels)] = 1
    gather, scatter = jnp.asarray(gather, BF16), jnp.asarray(gather.T, BF16)

    normed, source = sources(nodes, source_weight)
    edge = source.reshape(lat, levels, lon, width)
    west = lax.ppermute(edge[:, :, lon - 1], "sector", up)
    east = lax.ppermute(edge[:, :, 0], "sector", down)
    message = functools.partial(
        messages,
        levels=levels,
        normed=normed,
        source=source,
        nodes=nodes,
        target_w=target_weight,
        node_w=node_weight,
        bias=direction_bias,
    )
    far = {1: message((1,), order=far_rows)}
    far[0] = message((0,), order=far_rows, edges=(west, east))
    far[2] = message((2,), order=far_rows, edges=(west, east))
    own = message(tuple(range(blocks)), order=own_rows, edges=(west, east))

    near = lax.ppermute(own[:, 1], "level", sibling)
    done_own, done_sibling, done_opposite = {}, {}, {}
    for b in (1, 0, 2):
        arrived = lax.ppermute(far[b], "level", opposite)
        across = lax.ppermute(arrived[0, 1], "level", sibling)
        done_own[b], toward, beside = attention(
            b, own, arrived, near, across, bias, gather, scatter, query_key, value_weight, output_weight
        )
        done_sibling[b] = lax.ppermute(beside, "level", sibling)
        back = jnp.stack([toward, done_sibling[b][1]])
        done_opposite[b] = lax.ppermute(back, "level", opposite)
    place = here.reshape(1).astype(jnp.int32)
    listed = lambda d: [d[b] for b in range(blocks)]
    out = finish(levels, place, listed(done_own), listed(done_sibling), listed(done_opposite))
    return jnp.transpose(out.reshape(lat, levels, lon, width), (0, 2, 1, 3))


def solution(mesh):
    placed = (P(None, "sector", "level", None), P(), P(), P(), P(), P(), P(), P(), P())
    return jax.shard_map(
        per_device,
        mesh=mesh,
        in_specs=placed,
        out_specs=P(None, "sector", "level", None),
        check_vma=False,
    )
```

```python
import functools

import jax
import jax.numpy as jnp
from jax import lax
from jax.experimental import pallas as pl
from jax.experimental.pallas import tpu as pltpu
from jax.sharding import PartitionSpec as P

HEAD = 64
EPSILON = 1e-06
MASKED = -1e30
GROUP = 8
LANES = 128
HALF = GROUP // 2
F32, BF16 = jnp.float32, jnp.bfloat16
WHOLE = pl.BlockSpec(memory_space=pltpu.VMEM)
SCALARS = pl.BlockSpec(memory_space=pltpu.SMEM)
OUTSIDE = pl.BlockSpec(memory_space=pltpu.HBM)


def array(*shape, dtype=BF16):
    return jax.ShapeDtypeStruct(shape, dtype)


def params(mib=24):
    return pltpu.CompilerParams(vmem_limit_bytes=mib << 20)


def cost():
    return pl.CostEstimate(flops=1, bytes_accessed=1, transcendentals=0)


def normalize(x):
    return x * lax.rsqrt(jnp.mean(x * x, axis=-1, keepdims=True) + EPSILON)


def matmul(x, weight):
    return jnp.dot(x, weight, preferred_element_type=F32)


def place():
    here = lax.axis_index("level")
    return here // 2, here % 2


def chunk_of(x, chunk):
    first, middle, last = (x[:, GROUP * i : GROUP * (i + 1)] for i in range(3))
    if chunk == 0:
        return middle
    low = lax.broadcasted_iota(jnp.int32, first.shape, 1) < HALF
    return jnp.where(low, last, first) if chunk == 1 else jnp.where(low, first, last)


def whole_of(middle, beside, outer):
    low = lax.broadcasted_iota(jnp.int32, middle.shape, 1) < HALF
    return jnp.concatenate([jnp.where(low, outer, beside), middle, jnp.where(low, beside, outer)], axis=1)


def rows_of(ref, row, chunk, levels):
    lon = ref.shape[-2] // levels
    x = chunk_of(ref[row].astype(F32).reshape(levels, lon, ref.shape[-1]), chunk)
    return x.reshape(levels * GROUP, ref.shape[-1])


def update_pieces(pieces, levels, halves, target_w, node_w, bias_ref, edges, target_ref, sum_ref):
    chip, core = place()
    width = bias_ref.shape[-1]
    size = levels * GROUP
    lon = halves[0][0].shape[1] // levels
    side = [jnp.where(chip == (1 if far else 0), 0, 1) for far in (False, True)]
    x = [rows_of(halves[h][0], core + side[far], c, levels).astype(BF16) for far, c, h in pieces]
    target_ref[...] = matmul(jnp.concatenate(x, axis=0), target_w[...]) * 0.5
    step = LANES
    for n, (far, c, h) in enumerate(pieces):
        source_ref = halves[h][1]
        row = core + side[far]
        lat = core + row
        north, south = jnp.maximum(row - 1, 0), jnp.minimum(row + 1, 2)
        has_north = jnp.where(lat >= 1, 1.0, 0.0)
        has_south = jnp.where(lat <= 2, 1.0, 0.0)
        if c == 2:
            west_edge = edges[0][2 * h + side[far]].astype(F32)
            east_edge = edges[1][2 * h + side[far]].astype(F32)
        for pair in range(levels // 2):
            for lane in range(0, width, step):
                cols = slice(lane, lane + step)
                rows = slice(2 * lon * pair, 2 * lon * (pair + 1))
                at = slice(n * size + 2 * GROUP * pair, n * size + 2 * GROUP * (pair + 1))

                def take(x):
                    return chunk_of(x.reshape(2, lon, step), c).reshape(2 * GROUP, step)

                def put(x, place, edge):
                    place = lax.broadcasted_iota(jnp.int32, (GROUP, step), 0) == place
                    parts = [
                        jnp.where(place, edge[2 * pair + k : 2 * pair + k + 1, cols], x[GROUP * k : GROUP * (k + 1)])
                        for k in range(2)
                    ]
                    return jnp.concatenate(parts, axis=0)

                middle = source_ref[row, rows, cols].astype(F32)
                east = take(pltpu.roll(middle, 2 * lon - 1, 0))
                west = take(pltpu.roll(middle, 1, 0))
                if c == 2:
                    west = put(west, 0, west_edge)
                    east = put(east, GROUP - 1, east_edge)
                target = target_ref[at, cols]

                def halved_silu(other, k):
                    half = target + other + bias_ref[k : k + 1, cols]
                    return half + half * jnp.tanh(half)

                total = halved_silu(east, 0) + halved_silu(west, 1)
                other = take(source_ref[north, rows, cols].astype(F32))
                total = total + halved_silu(other, 2) * has_north
                other = take(source_ref[south, rows, cols].astype(F32))
                total = total + halved_silu(other, 3) * has_south
                sum_ref[at, cols] = total.astype(BF16)
    update = matmul(sum_ref[...], node_w[...])
    out = []
    for n, (far, c, h) in enumerate(pieces):
        nodes_ref, offset = halves[h][2:]
        own = rows_of(nodes_ref, offset + side[far], c, levels)
        out.append((own + update[n * size : (n + 1) * size]).astype(BF16))
    return out


def source_rows(read, normed_ref, source_ref, source_w):
    count, rows, _ = normed_ref.shape
    for i in range(count):
        normed_ref[i] = normalize(read(i).astype(F32)).astype(BF16)
    normed = jnp.concatenate([normed_ref[i] for i in range(count)], axis=0)
    source = (matmul(normed, source_w[...]) * 0.5).astype(BF16)
    for i in range(count):
        source_ref[i] = source[i * rows : (i + 1) * rows]


def first_kernel(nodes_in, source_in, nodes_ref, source_w, normed_ref, source_ref, sems):
    count = nodes_ref.shape[0]
    _, core = place()
    copies = [pltpu.make_async_copy(nodes_in.at[core + i], nodes_ref.at[i], sems.at[i]) for i in range(count)]
    copies.append(pltpu.make_async_copy(source_in, source_w, sems.at[count]))
    for copy in copies:
        copy.start()
    for copy in copies:
        copy.wait()
    source_rows(lambda i: nodes_ref[i], normed_ref, source_ref, source_w)


def outside(*arrays):
    return [pltpu.with_memory_space_constraint(x, pltpu.HBM) for x in arrays]


def first(nodes, source_w):
    lat, rows, width = nodes.shape
    three, square = array(3, rows, width), array(width, width)
    return pl.pallas_call(
        first_kernel,
        in_specs=[OUTSIDE] * 2,
        out_specs=[WHOLE] * 4,
        out_shape=[three, square, three, three],
        scratch_shapes=[pltpu.SemaphoreType.DMA((4,))],
        compiler_params=params(),
        cost_estimate=cost(),
    )(*outside(nodes, source_w))


def second_kernel(
    pieces, levels, target_in, node_in, bias_in, nodes_a, source_w, normed_a, source_a, nodes_b,
    target_w, node_w, bias_ref, normed_ref, source_ref, far_ref, target_ref, sum_ref, sems,
):
    _, core = place()
    copies = [
        pltpu.make_async_copy(*refs, sems.at[i])
        for i, refs in enumerate(((target_in, target_w), (node_in, node_w), (bias_in, bias_ref)))
    ]
    for copy in copies:
        copy.start()
    source_rows(lambda i: nodes_b[core + i], normed_ref, source_ref, source_w)
    for copy in copies:
        copy.wait()
    bias_ref[...] = bias_ref[...] * 0.5
    halves = ((normed_a, source_a, nodes_a, core), (normed_ref, source_ref, nodes_b, 2 * core))
    out = update_pieces(pieces, levels, halves, target_w, node_w, bias_ref, None, target_ref, sum_ref)
    far_ref[0], far_ref[1] = out


def second(levels, pieces, target_w, node_w, bias, *args):
    width = target_w.shape[0]
    three, square = array(*args[0].shape), array(width, width)
    size = levels * GROUP
    count = len(pieces) * size
    return pl.pallas_call(
        functools.partial(second_kernel, pieces, levels),
        in_specs=[OUTSIDE] * 3 + [WHOLE] * len(args),
        out_specs=[WHOLE] * 6,
        out_shape=[square, square, array(*bias.shape, dtype=F32), three, three, array(2, size, width)],
        scratch_shapes=[
            pltpu.VMEM((count, width), F32),
            pltpu.VMEM((count, width), BF16),
            pltpu.SemaphoreType.DMA((3,)),
        ],
        compiler_params=params(),
        cost_estimate=cost(),
    )(*outside(target_w, node_w, bias), *args)


def later_kernel(pieces, levels, with_edges, *refs):
    nodes_a, normed_a, source_a, nodes_b, normed_b, source_b, target_w, node_w, bias_ref = refs[:9]
    refs = refs[9:]
    _, core = place()
    edges = None
    if with_edges == "in":
        edges, refs = refs[:2], refs[2:]
    *outs, target_ref, sum_ref = refs
    if with_edges == "out":
        *outs, west_ref, east_ref, target_ref, sum_ref, edge_ref = refs
        lon = source_a.shape[1] // levels
        for h, source_ref in enumerate((source_a, source_b)):
            for k in range(2):
                source = source_ref[core + k].astype(F32)
                for level in range(levels):
                    edge_ref[0, level : level + 1] = source[level * lon : level * lon + 1]
                    edge_ref[1, level : level + 1] = source[(level + 1) * lon - 1 : (level + 1) * lon]
                east_ref[2 * h + k] = edge_ref[0].astype(BF16)
                west_ref[2 * h + k] = edge_ref[1].astype(BF16)
    halves = ((normed_a, source_a, nodes_a, core), (normed_b, source_b, nodes_b, 2 * core))
    out = update_pieces(pieces, levels, halves, target_w, node_w, bias_ref, edges, target_ref, sum_ref)
    for i, ref in enumerate(outs):
        ref[0], ref[1] = out[2 * i : 2 * i + 2]


def later(levels, pieces, shared, edges=None, with_edges=None):
    width = shared[0].shape[-1]
    size = levels * GROUP
    count = len(pieces) * size
    args = (*shared, *(edges or ()))
    shapes = [array(2, size, width)] * (len(pieces) // 2)
    scratch = [pltpu.VMEM((count, width), F32), pltpu.VMEM((count, width), BF16)]
    if with_edges == "out":
        shapes += [array(4, levels, width)] * 2
        scratch += [pltpu.VMEM((2, levels, width), F32)]
    return pl.pallas_call(
        functools.partial(later_kernel, pieces, levels, with_edges),
        in_specs=[WHOLE] * len(args),
        out_specs=[WHOLE] * len(shapes),
        out_shape=shapes,
        scratch_shapes=scratch,
        compiler_params=params(),
        cost_estimate=cost(),
    )(*args)


def attention_kernel(
    mask_ref, own_ref, opposite_ref, query_key, value_w, output_w,
    out_own, out_sibling, out_opposite, q_ref, k_ref, v_ref, att_ref, weight_ref, bias_ref,
):
    _, size, width = own_ref.shape
    here = lax.axis_index("level")
    levels = 4 * size // GROUP
    each = levels // 4
    tiles = width // LANES
    for q in range(4):
        for level in range(each):
            kept = jnp.where(mask_ref[(here ^ q) * each + level] > 0, 0.0, MASKED).astype(F32)
            bias_ref[q * each + level : q * each + level + 1] = jnp.full((1, LANES), kept)
    x = jnp.concatenate([own_ref[0], own_ref[1], opposite_ref[0], opposite_ref[1]], axis=0)
    normed = normalize(x.astype(F32)).astype(BF16)

    def spread(ref, y):
        for t in range(tiles):
            ref[t] = y[:, LANES * t : LANES * (t + 1)]

    spread(q_ref, matmul(normed, query_key[0]) * HEAD**-0.5)
    spread(k_ref, matmul(normed, query_key[1]))
    spread(v_ref, matmul(normed, value_w[...]))
    low = lax.broadcasted_iota(jnp.int32, (levels, LANES), 1) < HEAD
    pad = jnp.zeros((LANES - 2 * levels, LANES), BF16)
    bias = bias_ref[...]
    for column in range(GROUP):
        rows = pl.ds(column, levels, stride=GROUP)
        for t in range(tiles):
            query, key = q_ref[t, rows, :].astype(BF16), k_ref[t, rows, :].astype(BF16)
            zero = jnp.zeros_like(query)
            both = jnp.concatenate([jnp.where(low, query, zero), jnp.where(low, zero, query), pad], axis=0)
            scores = lax.dot_general(key, both, (((1,), (1,)), ((), ())), preferred_element_type=F32)
            scores = scores + bias
            weights = jnp.exp(scores - jnp.max(scores, axis=0, keepdims=True))
            weights = weights * (1.0 / jnp.sum(weights, axis=0, keepdims=True))
            weight_ref[levels * column : levels * (column + 1), LANES * t : LANES * (t + 1)] = weights.astype(BF16)
    for column in range(GROUP):
        rows = pl.ds(column, levels, stride=GROUP)
        for t in range(tiles):
            weights = weight_ref[levels * column : levels * (column + 1), LANES * t : LANES * (t + 1)]
            value = v_ref[t, rows, :].astype(BF16)
            mixed = lax.dot_general(weights, value, (((0,), (0,)), ((), ())), preferred_element_type=F32)
            att_ref[t, rows, :] = jnp.where(low, mixed[:levels], mixed[levels : 2 * levels])
    attended = jnp.concatenate([att_ref[t] for t in range(tiles)], axis=1).astype(BF16)
    out = (x.astype(F32) + matmul(attended, output_w[...])).astype(BF16)
    out_own[...] = out[:size]
    out_sibling[...] = out[size : 2 * size]
    out_opposite[0] = out[2 * size : 3 * size]
    out_opposite[1] = out[3 * size :]


def attention(*args):
    _, size, width = args[1].shape
    rows = 4 * size
    tiled = pltpu.VMEM((width // LANES, rows, LANES), F32)
    return pl.pallas_call(
        attention_kernel,
        in_specs=[SCALARS] + [WHOLE] * (len(args) - 1),
        out_specs=[WHOLE] * 3,
        out_shape=[array(size, width), array(size, width), array(2, size, width)],
        scratch_shapes=[tiled] * 4 + [pltpu.VMEM((rows, width), BF16), pltpu.VMEM((rows // GROUP, LANES), F32)],
        compiler_params=params(),
        cost_estimate=cost(),
    )(*args)


def finish_kernel(levels, targets, given, *refs):
    *pieces, out_ref, whole_ref, sems = refs[given:]
    chip, core = place()
    width = out_ref.shape[-1]
    lon = 3 * GROUP
    copies = []
    for n, (far, other) in enumerate(targets):
        for pair in range(levels // 2):
            rows = slice(2 * GROUP * pair, 2 * GROUP * (pair + 1))
            parts = [p[0][rows] if len(p.shape) == 3 else p[rows] for p in pieces[3 * n : 3 * n + 3]]
            whole = whole_of(*(p.astype(F32).reshape(2, GROUP, width) for p in parts))
            whole_ref[n, 2 * lon * pair : 2 * lon * (pair + 1)] = whole.reshape(2 * lon, width).astype(BF16)
        row = 2 * (1 - core if other else core) + (1 - chip if far else chip)
        copies.append(pltpu.make_async_copy(whole_ref.at[n], out_ref.at[row], sems.at[n]))
        copies[-1].start()
    for copy in copies:
        copy.wait()


def finish(levels, targets, shape, given, pieces):
    count = len(targets)
    return pl.pallas_call(
        functools.partial(finish_kernel, levels, targets, len(given)),
        in_specs=[OUTSIDE] * len(given) + [WHOLE] * len(pieces),
        out_specs=OUTSIDE,
        out_shape=array(*shape),
        input_output_aliases={0: 0} if given else {},
        scratch_shapes=[pltpu.VMEM((count, *shape[1:]), BF16), pltpu.SemaphoreType.DMA((count,))],
        compiler_params=params(),
        cost_estimate=cost(),
    )(*given, *pieces)


def after(x, *others):
    return lax.optimization_barrier((x, *others))[0]


def per_device(
    nodes, level_mask, source_weight, target_weight, direction_bias, node_weight, query_key, value_weight, output_weight
):
    lat, lon, levels, width = nodes.shape
    rows = levels * lon
    opposite = [(i, i ^ 2) for i in range(4)]
    sibling = [(i, i ^ 1) for i in range(4)]
    ring = lax.axis_size("sector")
    up = [(i, (i + 1) % ring) for i in range(ring)]
    down = [(j, i) for i, j in up]
    far_piece = lambda c: ((True, c, 0), (True, c, 1))
    own_piece = lambda c: ((False, c, 0), (False, c, 1))

    nodes = jnp.transpose(nodes, (0, 2, 1, 3)).reshape(lat, rows, width)
    nodes_b = lax.ppermute(nodes, "level", sibling)
    far, own = {}, {}
    nodes_a, source_w, normed_a, source_a = first(nodes, source_weight)
    target_w, node_w, bias, normed_b, source_b, far[0] = second(
        levels, far_piece(0), target_weight, node_weight, direction_bias, nodes_a, source_w, normed_a, source_a, nodes_b
    )
    shared = (nodes_a, normed_a, source_a, nodes_b, normed_b, source_b, target_w, node_w, bias)
    far[1], own[0], west, east = later(levels, far_piece(1) + own_piece(0), shared, with_edges="out")
    west = lax.ppermute(west, "sector", up)
    east = lax.ppermute(east, "sector", down)
    (own[1],) = later(levels, own_piece(1), (after(nodes_a, own[0]), *shared[1:]))
    far[2], own[2] = later(levels, far_piece(2) + own_piece(2), (after(nodes_a, own[1]), *shared[1:]), (west, east), "in")
    done, close, back, distant = {}, {}, {}, {}
    for c in range(3):
        arrived = lax.ppermute(far[c], "level", opposite)
        mine = own[0] if c == 0 else after(own[c], done[c - 1], *([back[0]] if c == 2 else []))
        args = (level_mask, mine, arrived, query_key, value_weight, output_weight)
        done[c], close[c], toward = attention(*args)
        back[c] = lax.ppermute(toward, "level", opposite)
    late = lambda x: after(x, done[2])
    close = {c: lax.ppermute(late(close[c]), "level", sibling) for c in range(3)}
    for c in range(2):
        distant[c] = lax.ppermute(late(back[c][1]), "level", sibling)
    shape = (lat, rows, width)
    listed = lambda d: [d[c] for c in range(3)]
    out = finish(levels, ((False, False), (False, True)), shape, (), listed(done) + listed(close))
    back[2] = after(back[2], out)
    distant[2] = lax.ppermute(back[2][1], "level", sibling)
    out = finish(levels, ((True, False),), shape, (out,), listed(back))
    out = finish(levels, ((True, True),), shape, (out,), listed(distant))
    return jnp.transpose(out.reshape(lat, levels, lon, width), (0, 2, 1, 3))


def solution(mesh):
    placed = (P(None, "sector", "level", None), P(), P(), P(), P(), P(), P(), P(), P())
    return jax.shard_map(
        per_device,
        mesh=mesh,
        in_specs=placed,
        out_specs=P(None, "sector", "level", None),
        check_vma=False,
    )
```

```python
import functools

import jax
import jax.numpy as jnp
from jax import lax
from jax.experimental import pallas as pl
from jax.experimental.pallas import tpu as pltpu
from jax.sharding import PartitionSpec as P

HEAD = 64
EPSILON = 1e-06
MASKED = -1e30
GROUP = 8
LANES = 128
HALF = GROUP // 2
F32, BF16 = jnp.float32, jnp.bfloat16
WHOLE = pl.BlockSpec(memory_space=pltpu.VMEM)
SCALARS = pl.BlockSpec(memory_space=pltpu.SMEM)
OUTSIDE = pl.BlockSpec(memory_space=pltpu.HBM)


def array(*shape, dtype=BF16):
    return jax.ShapeDtypeStruct(shape, dtype)


def params(mib=24):
    return pltpu.CompilerParams(vmem_limit_bytes=mib << 20)


def cost():
    return pl.CostEstimate(flops=1, bytes_accessed=1, transcendentals=0)


def normalize(x):
    return x * lax.rsqrt(jnp.mean(x * x, axis=-1, keepdims=True) + EPSILON)


def matmul(x, weight):
    return jnp.dot(x, weight, preferred_element_type=F32)


def place():
    here = lax.axis_index("level")
    return here // 2, here % 2


def chunk_of(x, chunk):
    first, middle, last = (x[:, GROUP * i : GROUP * (i + 1)] for i in range(3))
    if chunk == 0:
        return middle
    low = lax.broadcasted_iota(jnp.int32, first.shape, 1) < HALF
    return jnp.where(low, last, first) if chunk == 1 else jnp.where(low, first, last)


def whole_of(middle, beside, outer):
    low = lax.broadcasted_iota(jnp.int32, middle.shape, 1) < HALF
    return jnp.concatenate([jnp.where(low, outer, beside), middle, jnp.where(low, beside, outer)], axis=1)


def rows_of(ref, row, chunk, levels):
    lon = ref.shape[-2] // levels
    x = chunk_of(ref[row].astype(F32).reshape(levels, lon, ref.shape[-1]), chunk)
    return x.reshape(levels * GROUP, ref.shape[-1])


def update_pieces(pieces, levels, halves, target_w, node_w, bias_ref, edges, target_ref, sum_ref):
    chip, core = place()
    width = bias_ref.shape[-1]
    size = levels * GROUP
    lon = halves[0][0].shape[1] // levels
    side = [jnp.where(chip == (1 if far else 0), 0, 1) for far in (False, True)]
    x = [rows_of(halves[h][0], core + side[far], c, levels).astype(BF16) for far, c, h in pieces]
    target_ref[...] = matmul(jnp.concatenate(x, axis=0), target_w[...]) * 0.5
    step = LANES
    for n, (far, c, h) in enumerate(pieces):
        source_ref = halves[h][1]
        row = core + side[far]
        lat = core + row
        north, south = jnp.maximum(row - 1, 0), jnp.minimum(row + 1, 2)
        has_north = jnp.where(lat >= 1, 1.0, 0.0)
        has_south = jnp.where(lat <= 2, 1.0, 0.0)
        if c == 2:
            west_edge = edges[0][2 * h + side[far]].astype(F32)
            east_edge = edges[1][2 * h + side[far]].astype(F32)
        for pair in range(levels // 2):
            for lane in range(0, width, step):
                cols = slice(lane, lane + step)
                rows = slice(2 * lon * pair, 2 * lon * (pair + 1))
                at = slice(n * size + 2 * GROUP * pair, n * size + 2 * GROUP * (pair + 1))

                def take(x):
                    return chunk_of(x.reshape(2, lon, step), c).reshape(2 * GROUP, step)

                def put(x, place, edge):
                    place = lax.broadcasted_iota(jnp.int32, (GROUP, step), 0) == place
                    parts = [
                        jnp.where(place, edge[2 * pair + k : 2 * pair + k + 1, cols], x[GROUP * k : GROUP * (k + 1)])
                        for k in range(2)
                    ]
                    return jnp.concatenate(parts, axis=0)

                middle = source_ref[row, rows, cols].astype(F32)
                east = take(pltpu.roll(middle, 2 * lon - 1, 0))
                west = take(pltpu.roll(middle, 1, 0))
                if c == 2:
                    west = put(west, 0, west_edge)
                    east = put(east, GROUP - 1, east_edge)
                target = target_ref[at, cols]

                def halved_silu(other, k):
                    half = target + other + bias_ref[k : k + 1, cols]
                    return half + half * jnp.tanh(half)

                total = halved_silu(east, 0) + halved_silu(west, 1)
                other = take(source_ref[north, rows, cols].astype(F32))
                total = total + halved_silu(other, 2) * has_north
                other = take(source_ref[south, rows, cols].astype(F32))
                total = total + halved_silu(other, 3) * has_south
                sum_ref[at, cols] = total.astype(BF16)
    update = matmul(sum_ref[...], node_w[...])
    out = []
    for n, (far, c, h) in enumerate(pieces):
        nodes_ref, offset = halves[h][2:]
        own = rows_of(nodes_ref, offset + side[far], c, levels)
        out.append((own + update[n * size : (n + 1) * size]).astype(BF16))
    return out


def source_rows(read, normed_ref, source_ref, source_w):
    count, rows, _ = normed_ref.shape
    for i in range(count):
        normed_ref[i] = normalize(read(i).astype(F32)).astype(BF16)
    normed = jnp.concatenate([normed_ref[i] for i in range(count)], axis=0)
    source = (matmul(normed, source_w[...]) * 0.5).astype(BF16)
    for i in range(count):
        source_ref[i] = source[i * rows : (i + 1) * rows]


def first_kernel(
    nodes_in, source_in, target_in, node_in, bias_in,
    nodes_ref, target_w, node_w, bias_ref, source_w, normed_ref, source_ref, sems,
):
    count = nodes_ref.shape[0]
    _, core = place()
    pairs = [(nodes_in.at[core + i], nodes_ref.at[i]) for i in range(count)]
    pairs += [(source_in, source_w), (target_in, target_w), (node_in, node_w), (bias_in, bias_ref)]
    copies = [pltpu.make_async_copy(*pair, sems.at[i]) for i, pair in enumerate(pairs)]
    for copy in copies:
        copy.start()
    for copy in copies[: count + 1]:
        copy.wait()
    source_rows(lambda i: nodes_ref[i], normed_ref, source_ref, source_w)
    for copy in copies[count + 1 :]:
        copy.wait()
    bias_ref[...] = bias_ref[...] * 0.5


def outside(*arrays):
    return [pltpu.with_memory_space_constraint(x, pltpu.HBM) for x in arrays]


def first(nodes, source_w, target_w, node_w, bias):
    lat, rows, width = nodes.shape
    three, square = array(3, rows, width), array(width, width)
    return pl.pallas_call(
        first_kernel,
        in_specs=[OUTSIDE] * 5,
        out_specs=[WHOLE] * 7,
        out_shape=[three, square, square, array(*bias.shape, dtype=F32), square, three, three],
        scratch_shapes=[pltpu.SemaphoreType.DMA((7,))],
        compiler_params=params(),
        cost_estimate=cost(),
    )(*outside(nodes, source_w, target_w, node_w, bias))


def second_kernel(
    pieces, levels, nodes_a, target_w, node_w, bias_ref, source_w, normed_a, source_a, nodes_b,
    normed_ref, source_ref, far_ref, target_ref, sum_ref,
):
    _, core = place()
    source_rows(lambda i: nodes_b[core + i], normed_ref, source_ref, source_w)
    halves = ((normed_a, source_a, nodes_a, core), (normed_ref, source_ref, nodes_b, 2 * core))
    out = update_pieces(pieces, levels, halves, target_w, node_w, bias_ref, None, target_ref, sum_ref)
    far_ref[0], far_ref[1] = out


def second(levels, pieces, *args):
    three = array(*args[0].shape)
    width = three.shape[-1]
    size = levels * GROUP
    count = len(pieces) * size
    return pl.pallas_call(
        functools.partial(second_kernel, pieces, levels),
        in_specs=[WHOLE] * len(args),
        out_specs=[WHOLE] * 3,
        out_shape=[three, three, array(2, size, width)],
        scratch_shapes=[pltpu.VMEM((count, width), F32), pltpu.VMEM((count, width), BF16)],
        compiler_params=params(),
        cost_estimate=cost(),
    )(*args)


def later_kernel(pieces, levels, with_edges, *refs):
    nodes_a, normed_a, source_a, nodes_b, normed_b, source_b, target_w, node_w, bias_ref = refs[:9]
    refs = refs[9:]
    _, core = place()
    edges = None
    if with_edges == "in":
        edges, refs = refs[:2], refs[2:]
    *outs, target_ref, sum_ref = refs
    if with_edges == "out":
        mask_ref, *outs, west_ref, east_ref, kept_ref, target_ref, sum_ref, edge_ref = refs
        here = lax.axis_index("level")
        for q in range(4):
            for level in range(levels):
                kept = jnp.where(mask_ref[(here ^ q) * levels + level] > 0, 0.0, MASKED).astype(F32)
                kept_ref[q * levels + level : q * levels + level + 1] = jnp.full((1, LANES), kept)
        lon = source_a.shape[1] // levels
        for h, source_ref in enumerate((source_a, source_b)):
            for k in range(2):
                source = source_ref[core + k].astype(F32)
                for level in range(levels):
                    edge_ref[0, level : level + 1] = source[level * lon : level * lon + 1]
                    edge_ref[1, level : level + 1] = source[(level + 1) * lon - 1 : (level + 1) * lon]
                east_ref[2 * h + k] = edge_ref[0].astype(BF16)
                west_ref[2 * h + k] = edge_ref[1].astype(BF16)
    halves = ((normed_a, source_a, nodes_a, core), (normed_b, source_b, nodes_b, 2 * core))
    out = update_pieces(pieces, levels, halves, target_w, node_w, bias_ref, edges, target_ref, sum_ref)
    for i, ref in enumerate(outs):
        ref[0], ref[1] = out[2 * i : 2 * i + 2]


def later(levels, pieces, shared, more=(), with_edges=None):
    width = shared[0].shape[-1]
    size = levels * GROUP
    count = len(pieces) * size
    args = (*shared, *more)
    specs = [WHOLE] * len(args)
    shapes = [array(2, size, width)] * (len(pieces) // 2)
    scratch = [pltpu.VMEM((count, width), F32), pltpu.VMEM((count, width), BF16)]
    if with_edges == "out":
        specs[-1] = SCALARS
        shapes += [array(4, levels, width)] * 2 + [array(4 * levels, LANES, dtype=F32)]
        scratch += [pltpu.VMEM((2, levels, width), F32)]
    return pl.pallas_call(
        functools.partial(later_kernel, pieces, levels, with_edges),
        in_specs=specs,
        out_specs=[WHOLE] * len(shapes),
        out_shape=shapes,
        scratch_shapes=scratch,
        compiler_params=params(),
        cost_estimate=cost(),
    )(*args)


def attention_kernel(
    kept_ref, own_ref, opposite_ref, query_key, value_w, output_w,
    out_own, out_sibling, out_opposite, q_ref, k_ref, v_ref, att_ref, weight_ref,
):
    _, size, width = own_ref.shape
    levels = 4 * size // GROUP
    tiles = width // LANES
    x = jnp.concatenate([own_ref[0], own_ref[1], opposite_ref[0], opposite_ref[1]], axis=0)
    normed = normalize(x.astype(F32)).astype(BF16)

    def spread(ref, y):
        for t in range(tiles):
            ref[t] = y[:, LANES * t : LANES * (t + 1)]

    spread(q_ref, matmul(normed, query_key[0]) * HEAD**-0.5)
    spread(k_ref, matmul(normed, query_key[1]))
    spread(v_ref, matmul(normed, value_w[...]))
    low = lax.broadcasted_iota(jnp.int32, (levels, LANES), 1) < HEAD
    pad = jnp.zeros((LANES - 2 * levels, LANES), BF16)
    kept = kept_ref[...]
    for column in range(GROUP):
        rows = pl.ds(column, levels, stride=GROUP)
        for t in range(tiles):
            query, key = q_ref[t, rows, :].astype(BF16), k_ref[t, rows, :].astype(BF16)
            zero = jnp.zeros_like(query)
            both = jnp.concatenate([jnp.where(low, query, zero), jnp.where(low, zero, query), pad], axis=0)
            scores = lax.dot_general(key, both, (((1,), (1,)), ((), ())), preferred_element_type=F32)
            scores = scores + kept
            weights = jnp.exp(scores - jnp.max(scores, axis=0, keepdims=True))
            weights = weights * (1.0 / jnp.sum(weights, axis=0, keepdims=True))
            weight_ref[levels * column : levels * (column + 1), LANES * t : LANES * (t + 1)] = weights.astype(BF16)
    for column in range(GROUP):
        rows = pl.ds(column, levels, stride=GROUP)
        for t in range(tiles):
            weights = weight_ref[levels * column : levels * (column + 1), LANES * t : LANES * (t + 1)]
            value = v_ref[t, rows, :].astype(BF16)
            mixed = lax.dot_general(weights, value, (((0,), (0,)), ((), ())), preferred_element_type=F32)
            att_ref[t, rows, :] = jnp.where(low, mixed[:levels], mixed[levels : 2 * levels])
    attended = jnp.concatenate([att_ref[t] for t in range(tiles)], axis=1).astype(BF16)
    out = (x.astype(F32) + matmul(attended, output_w[...])).astype(BF16)
    out_own[...] = out[:size]
    out_sibling[...] = out[size : 2 * size]
    out_opposite[0] = out[2 * size : 3 * size]
    out_opposite[1] = out[3 * size :]


def attention(*args):
    _, size, width = args[1].shape
    rows = 4 * size
    tiled = pltpu.VMEM((width // LANES, rows, LANES), F32)
    return pl.pallas_call(
        attention_kernel,
        in_specs=[WHOLE] * len(args),
        out_specs=[WHOLE] * 3,
        out_shape=[array(size, width), array(size, width), array(2, size, width)],
        scratch_shapes=[tiled] * 4 + [pltpu.VMEM((rows, width), BF16)],
        compiler_params=params(),
        cost_estimate=cost(),
    )(*args)


def finish_kernel(levels, targets, given, *refs):
    *pieces, out_ref, whole_ref, sems = refs[given:]
    chip, core = place()
    width = out_ref.shape[-1]
    lon = 3 * GROUP
    copies = []
    for n, (far, other) in enumerate(targets):
        for pair in range(levels // 2):
            rows = slice(2 * GROUP * pair, 2 * GROUP * (pair + 1))
            parts = [p[0][rows] if len(p.shape) == 3 else p[rows] for p in pieces[3 * n : 3 * n + 3]]
            whole = whole_of(*(p.astype(F32).reshape(2, GROUP, width) for p in parts))
            whole_ref[n, 2 * lon * pair : 2 * lon * (pair + 1)] = whole.reshape(2 * lon, width).astype(BF16)
        row = 2 * (1 - core if other else core) + (1 - chip if far else chip)
        copies.append(pltpu.make_async_copy(whole_ref.at[n], out_ref.at[row], sems.at[n]))
        copies[-1].start()
    for copy in copies:
        copy.wait()


def finish(levels, targets, shape, given, pieces):
    count = len(targets)
    return pl.pallas_call(
        functools.partial(finish_kernel, levels, targets, len(given)),
        in_specs=[OUTSIDE] * len(given) + [WHOLE] * len(pieces),
        out_specs=OUTSIDE,
        out_shape=array(*shape),
        input_output_aliases={0: 0} if given else {},
        scratch_shapes=[pltpu.VMEM((count, *shape[1:]), BF16), pltpu.SemaphoreType.DMA((count,))],
        compiler_params=params(),
        cost_estimate=cost(),
    )(*given, *pieces)


def after(x, *others):
    return lax.optimization_barrier((x, *others))[0]


def per_device(
    nodes, level_mask, source_weight, target_weight, direction_bias, node_weight, query_key, value_weight, output_weight
):
    lat, lon, levels, width = nodes.shape
    rows = levels * lon
    opposite = [(i, i ^ 2) for i in range(4)]
    sibling = [(i, i ^ 1) for i in range(4)]
    ring = lax.axis_size("sector")
    up = [(i, (i + 1) % ring) for i in range(ring)]
    down = [(j, i) for i, j in up]
    far_piece = lambda c: ((True, c, 0), (True, c, 1))
    own_piece = lambda c: ((False, c, 0), (False, c, 1))

    nodes = jnp.transpose(nodes, (0, 2, 1, 3)).reshape(lat, rows, width)
    nodes_b = lax.ppermute(nodes, "level", sibling)
    far, own = {}, {}
    nodes_a, target_w, node_w, bias, source_w, normed_a, source_a = first(
        nodes, source_weight, target_weight, node_weight, direction_bias
    )
    normed_b, source_b, far[0] = second(
        levels, far_piece(0), nodes_a, target_w, node_w, bias, source_w, normed_a, source_a, nodes_b
    )
    shared = (nodes_a, normed_a, source_a, nodes_b, normed_b, source_b, target_w, node_w, bias)
    far[1], west, east, kept = later(levels, far_piece(1), shared, (level_mask,), "out")
    west = lax.ppermute(west, "sector", up)
    east = lax.ppermute(east, "sector", down)
    then = lambda x: (after(nodes_a, x), *shared[1:])
    (own[0],) = later(levels, own_piece(0), then(far[1]))
    (far[2],) = later(levels, far_piece(2), then(own[0]), (west, east), "in")
    done, close, back, distant = {}, {}, {}, {}
    for c in range(3):
        arrived = lax.ppermute(far[c], "level", opposite)
        if c == 1:
            own[1], own[2] = later(levels, own_piece(1) + own_piece(2), then(done[0]), (west, east), "in")
        mine = after(own[c], far[2] if c == 0 else done[c - 1])
        args = (kept, mine, arrived, query_key, value_weight, output_weight)
        done[c], close[c], toward = attention(*args)
        if c == 2:
            toward = after(toward, back[0])
        back[c] = lax.ppermute(toward, "level", opposite)
    late = lambda x: after(x, done[2], back[0])
    close = {c: lax.ppermute(late(close[c]), "level", sibling) for c in range(3)}
    for c in range(2):
        distant[c] = lax.ppermute(late(back[c][1]), "level", sibling)
    shape = (lat, rows, width)
    listed = lambda d: [d[c] for c in range(3)]
    out = finish(levels, ((False, False), (False, True)), shape, (), listed(done) + listed(close))
    back[2] = after(back[2], out)
    distant[2] = lax.ppermute(back[2][1], "level", sibling)
    out = finish(levels, ((True, False),), shape, (out,), listed(back))
    out = finish(levels, ((True, True),), shape, (out,), listed(distant))
    return jnp.transpose(out.reshape(lat, levels, lon, width), (0, 2, 1, 3))


def solution(mesh):
    placed = (P(None, "sector", "level", None), P(), P(), P(), P(), P(), P(), P(), P())
    return jax.shard_map(
        per_device,
        mesh=mesh,
        in_specs=placed,
        out_specs=P(None, "sector", "level", None),
        check_vma=False,
    )
```

```python
import functools

import jax
import jax.numpy as jnp
from jax import lax
from jax.experimental import pallas as pl
from jax.experimental.pallas import tpu as pltpu
from jax.sharding import PartitionSpec as P

HEAD = 64
EPSILON = 1e-06
MASKED = -1e30
GROUP = 8
LANES = 128
HALF = GROUP // 2
F32, BF16 = jnp.float32, jnp.bfloat16
WHOLE = pl.BlockSpec(memory_space=pltpu.VMEM)
SCALARS = pl.BlockSpec(memory_space=pltpu.SMEM)
OUTSIDE = pl.BlockSpec(memory_space=pltpu.HBM)


def array(*shape, dtype=BF16):
    return jax.ShapeDtypeStruct(shape, dtype)


def params(mib=24):
    return pltpu.CompilerParams(vmem_limit_bytes=mib << 20)


def cost(flops=1):
    return pl.CostEstimate(flops=flops, bytes_accessed=1, transcendentals=0)


def normalize(x):
    return x * lax.rsqrt(jnp.mean(x * x, axis=-1, keepdims=True) + EPSILON)


def matmul(x, weight):
    return jnp.dot(x, weight, preferred_element_type=F32)


def place():
    here = lax.axis_index("level")
    return here // 2, here % 2


def chunk_of(x, chunk):
    first, middle, last = (x[:, GROUP * i : GROUP * (i + 1)] for i in range(3))
    if chunk == 0:
        return middle
    low = lax.broadcasted_iota(jnp.int32, first.shape, 1) < HALF
    return jnp.where(low, last, first) if chunk == 1 else jnp.where(low, first, last)


def whole_of(middle, beside, outer):
    low = lax.broadcasted_iota(jnp.int32, middle.shape, 1) < HALF
    return jnp.concatenate([jnp.where(low, outer, beside), middle, jnp.where(low, beside, outer)], axis=1)


def by_chunk(x, levels):
    rows, width = x.shape
    x = x.astype(F32).reshape(levels, rows // levels, width)
    return jnp.concatenate([chunk_of(x, c).reshape(levels * GROUP, width) for c in range(3)], axis=0)


def update_pieces(pieces, levels, halves, target_w, node_w, bias_ref, edges, target_ref, sum_ref):
    chip, core = place()
    width = bias_ref.shape[-1]
    size = levels * GROUP
    side = [jnp.where(chip == (1 if far else 0), 0, 1) for far in (False, True)]
    x = [halves[h][0][core + side[far], size * c : size * (c + 1)] for far, c, h in pieces]
    target_ref[...] = matmul(jnp.concatenate(x, axis=0), target_w[...]) * 0.5
    step = LANES
    for n, (far, c, h) in enumerate(pieces):
        _, source_ref, east_ref, west_ref = halves[h][:4]
        row = core + side[far]
        lat = core + row
        north, south = jnp.maximum(row - 1, 0), jnp.minimum(row + 1, 2)
        has_north = jnp.where(lat >= 1, 1.0, 0.0)
        has_south = jnp.where(lat <= 2, 1.0, 0.0)
        if c == 2:
            west_edge = edges[0][2 * h + side[far]].astype(F32)
            east_edge = edges[1][2 * h + side[far]].astype(F32)
        for pair in range(levels // 2):
            for lane in range(0, width, step):
                cols = slice(lane, lane + step)
                rows = slice(size * c + 2 * GROUP * pair, size * c + 2 * GROUP * (pair + 1))
                at = slice(n * size + 2 * GROUP * pair, n * size + 2 * GROUP * (pair + 1))

                def put(x, place, edge):
                    place = lax.broadcasted_iota(jnp.int32, (GROUP, step), 0) == place
                    parts = [
                        jnp.where(place, edge[2 * pair + k : 2 * pair + k + 1, cols], x[GROUP * k : GROUP * (k + 1)])
                        for k in range(2)
                    ]
                    return jnp.concatenate(parts, axis=0)

                east = east_ref[side[far], rows, cols].astype(F32)
                west = west_ref[side[far], rows, cols].astype(F32)
                if c == 2:
                    west = put(west, 0, west_edge)
                    east = put(east, GROUP - 1, east_edge)
                target = target_ref[at, cols]

                def halved_silu(other, k):
                    half = target + other + bias_ref[k : k + 1, cols]
                    return half + half * jnp.tanh(half)

                total = halved_silu(east, 0) + halved_silu(west, 1)
                total = total + halved_silu(source_ref[north, rows, cols].astype(F32), 2) * has_north
                total = total + halved_silu(source_ref[south, rows, cols].astype(F32), 3) * has_south
                sum_ref[at, cols] = total.astype(BF16)
    update = matmul(sum_ref[...], node_w[...])
    out = []
    for n, (far, c, h) in enumerate(pieces):
        nodes_ref, offset = halves[h][4:]
        lon = nodes_ref.shape[1] // levels
        own = nodes_ref[offset + side[far]].astype(F32).reshape(levels, lon, width)
        own = chunk_of(own, c).reshape(size, width)
        out.append((own + update[n * size : (n + 1) * size]).astype(BF16))
    return out


def source_rows(levels, read, normed_ref, source_ref, east_ref, west_ref, raw_ref, edges, source_w):
    _, core = place()
    count, rows, width = normed_ref.shape
    size = levels * GROUP
    for i in range(count):
        normed_ref[i] = normalize(by_chunk(read(i), levels)).astype(BF16)
    normed = jnp.concatenate([normed_ref[i] for i in range(count)], axis=0)
    source = matmul(normed, source_w[...]) * 0.5
    for i in range(count):
        raw_ref[i] = source[i * rows : (i + 1) * rows]
        source_ref[i] = source[i * rows : (i + 1) * rows].astype(BF16)
    shape = (2, GROUP, LANES)
    spot = lax.broadcasted_iota(jnp.int32, shape, 1)
    for k in range(2):
        for pair in range(levels // 2):
            for lane in range(0, width, LANES):
                cols = slice(lane, lane + LANES)
                at = [slice(size * c + 2 * GROUP * pair, size * c + 2 * GROUP * (pair + 1)) for c in range(3)]
                x = [raw_ref[core + k, at[c], cols].reshape(shape) for c in range(3)]
                up = [pltpu.roll(y, GROUP - 1, 1) for y in x]
                down = [pltpu.roll(y, 1, 1) for y in x]
                last, half = spot == GROUP - 1, spot == HALF - 1
                east = [
                    jnp.where(last, up[1], up[0]),
                    jnp.where(half, up[2], jnp.where(last, up[0], up[1])),
                    jnp.where(half, up[1], up[2]),
                ]
                first, half = spot == 0, spot == HALF
                west = [
                    jnp.where(first, down[1], down[0]),
                    jnp.where(half, down[2], jnp.where(first, down[0], down[1])),
                    jnp.where(half, down[1], down[2]),
                ]
                for c in range(3):
                    east_ref[k, at[c], cols] = east[c].reshape(2 * GROUP, LANES).astype(BF16)
                    west_ref[k, at[c], cols] = west[c].reshape(2 * GROUP, LANES).astype(BF16)
        for level in range(levels):
            at = 2 * size + level * GROUP
            edges[0][k, level : level + 1] = raw_ref[core + k, at : at + 1]
            edges[1][k, level : level + 1] = raw_ref[core + k, at + GROUP - 1 : at + GROUP]


def first_kernel(
    levels, nodes_in, source_in, target_in, node_in, bias_in,
    nodes_ref, target_w, node_w, bias_ref, source_w, normed_ref, source_ref, east_ref, west_ref, begin_ref, end_ref,
    raw_ref, sems,
):
    count = nodes_ref.shape[0]
    _, core = place()
    pairs = [(nodes_in.at[core + i], nodes_ref.at[i]) for i in range(count)]
    pairs += [(source_in, source_w), (target_in, target_w), (node_in, node_w), (bias_in, bias_ref)]
    copies = [pltpu.make_async_copy(*pair, sems.at[i]) for i, pair in enumerate(pairs)]
    for copy in copies:
        copy.start()
    for copy in copies[: count + 1]:
        copy.wait()
    source_rows(
        levels, lambda i: nodes_ref[i], normed_ref, source_ref, east_ref, west_ref, raw_ref, (begin_ref, end_ref), source_w
    )
    for copy in copies[count + 1 :]:
        copy.wait()
    bias_ref[...] = bias_ref[...] * 0.5


def outside(*arrays):
    return [pltpu.with_memory_space_constraint(x, pltpu.HBM) for x in arrays]


def first(levels, nodes, source_w, target_w, node_w, bias):
    lat, rows, width = nodes.shape
    three, two, square = array(3, rows, width), array(2, rows, width), array(width, width)
    edge = array(2, levels, width, dtype=F32)
    return pl.pallas_call(
        functools.partial(first_kernel, levels),
        in_specs=[OUTSIDE] * 5,
        out_specs=[WHOLE] * 11,
        out_shape=[three, square, square, array(*bias.shape, dtype=F32), square, three, three, two, two, edge, edge],
        scratch_shapes=[pltpu.VMEM((3, rows, width), F32), pltpu.SemaphoreType.DMA((7,))],
        compiler_params=params(),
        cost_estimate=cost(),
    )(*outside(nodes, source_w, target_w, node_w, bias))


def second_kernel(
    pieces, levels, nodes_a, target_w, node_w, bias_ref, source_w, normed_a, source_a, east_a, west_a, begin_a, end_a, nodes_b,
    normed_ref, source_ref, east_ref, west_ref, to_west_ref, to_east_ref, far_ref,
    raw_ref, begin_ref, end_ref, target_ref, sum_ref,
):
    _, core = place()
    source_rows(
        levels, lambda i: nodes_b[core + i], normed_ref, source_ref, east_ref, west_ref, raw_ref, (begin_ref, end_ref), source_w
    )
    for k in range(2):
        to_west_ref[k], to_west_ref[2 + k] = begin_a[k].astype(BF16), begin_ref[k].astype(BF16)
        to_east_ref[k], to_east_ref[2 + k] = end_a[k].astype(BF16), end_ref[k].astype(BF16)
    halves = (
        (normed_a, source_a, east_a, west_a, nodes_a, core),
        (normed_ref, source_ref, east_ref, west_ref, nodes_b, 2 * core),
    )
    out = update_pieces(pieces, levels, halves, target_w, node_w, bias_ref, None, target_ref, sum_ref)
    far_ref[0], far_ref[1] = out


def second(levels, pieces, *args):
    rows, width = args[0].shape[1:]
    three, two, edge = array(3, rows, width), array(2, rows, width), array(4, levels, width)
    size = levels * GROUP
    count = len(pieces) * size
    return pl.pallas_call(
        functools.partial(second_kernel, pieces, levels),
        in_specs=[WHOLE] * len(args),
        out_specs=[WHOLE] * 7,
        out_shape=[three, three, two, two, edge, edge, array(2, size, width)],
        scratch_shapes=[pltpu.VMEM((3, rows, width), F32)]
        + [pltpu.VMEM((2, levels, width), F32)] * 2
        + [pltpu.VMEM((count, width), F32), pltpu.VMEM((count, width), BF16)],
        compiler_params=params(),
        cost_estimate=cost(),
    )(*args)


def later_kernel(pieces, levels, has, *refs):
    nodes_a, normed_a, source_a, east_a, west_a, nodes_b, normed_b, source_b, east_b, west_b = refs[:10]
    target_w, node_w, bias_ref = refs[10:13]
    refs = refs[13:]
    _, core = place()
    edges = None
    if has == "edges":
        edges, refs = refs[:2], refs[2:]
    *outs, target_ref, sum_ref = refs
    if has == "mask":
        mask_ref, *outs, kept_ref = outs
        here = lax.axis_index("level")
        for q in range(4):
            for level in range(levels):
                kept = jnp.where(mask_ref[(here ^ q) * levels + level] > 0, 0.0, MASKED).astype(F32)
                kept_ref[q * levels + level : q * levels + level + 1] = jnp.full((1, LANES), kept)
    halves = (
        (normed_a, source_a, east_a, west_a, nodes_a, core),
        (normed_b, source_b, east_b, west_b, nodes_b, 2 * core),
    )
    out = update_pieces(pieces, levels, halves, target_w, node_w, bias_ref, edges, target_ref, sum_ref)
    for i, ref in enumerate(outs):
        ref[0], ref[1] = out[2 * i : 2 * i + 2]


def later(levels, pieces, shared, more=(), has=None):
    width = shared[0].shape[-1]
    size = levels * GROUP
    count = len(pieces) * size
    args = (*shared, *more)
    specs = [WHOLE] * len(args)
    shapes = [array(2, size, width)] * (len(pieces) // 2)
    if has == "mask":
        specs[-1] = SCALARS
        shapes += [array(4 * levels, LANES, dtype=F32)]
    return pl.pallas_call(
        functools.partial(later_kernel, pieces, levels, has),
        in_specs=specs,
        out_specs=[WHOLE] * len(shapes),
        out_shape=shapes,
        scratch_shapes=[pltpu.VMEM((count, width), F32), pltpu.VMEM((count, width), BF16)],
        compiler_params=params(),
        cost_estimate=cost(),
    )(*args)


def attention_kernel(
    kept_ref, own_ref, opposite_ref, query_key, value_w, output_w,
    out_own, out_sibling, *refs,
):
    *out_opposite, q_ref, k_ref, v_ref, att_ref, weight_ref = refs
    _, size, width = own_ref.shape
    levels = 4 * size // GROUP
    tiles = width // LANES
    x = jnp.concatenate([own_ref[0], own_ref[1], opposite_ref[0], opposite_ref[1]], axis=0)
    normed = normalize(x.astype(F32)).astype(BF16)

    def spread(ref, y):
        for t in range(tiles):
            ref[t] = y[:, LANES * t : LANES * (t + 1)]

    spread(q_ref, matmul(normed, query_key[0]) * HEAD**-0.5)
    spread(k_ref, matmul(normed, query_key[1]))
    spread(v_ref, matmul(normed, value_w[...]))
    low = lax.broadcasted_iota(jnp.int32, (levels, LANES), 1) < HEAD
    pad = jnp.zeros((LANES - 2 * levels, LANES), BF16)
    kept = kept_ref[...]
    for column in range(GROUP):
        rows = pl.ds(column, levels, stride=GROUP)
        for t in range(tiles):
            query, key = q_ref[t, rows, :].astype(BF16), k_ref[t, rows, :].astype(BF16)
            zero = jnp.zeros_like(query)
            both = jnp.concatenate([jnp.where(low, query, zero), jnp.where(low, zero, query), pad], axis=0)
            scores = lax.dot_general(key, both, (((1,), (1,)), ((), ())), preferred_element_type=F32)
            scores = scores + kept
            weights = jnp.exp(scores - jnp.max(scores, axis=0, keepdims=True))
            weights = weights * (1.0 / jnp.sum(weights, axis=0, keepdims=True))
            weight_ref[levels * column : levels * (column + 1), LANES * t : LANES * (t + 1)] = weights.astype(BF16)
    for column in range(GROUP):
        rows = pl.ds(column, levels, stride=GROUP)
        for t in range(tiles):
            weights = weight_ref[levels * column : levels * (column + 1), LANES * t : LANES * (t + 1)]
            value = v_ref[t, rows, :].astype(BF16)
            mixed = lax.dot_general(weights, value, (((0,), (0,)), ((), ())), preferred_element_type=F32)
            att_ref[t, rows, :] = jnp.where(low, mixed[:levels], mixed[levels : 2 * levels])
    attended = jnp.concatenate([att_ref[t] for t in range(tiles)], axis=1).astype(BF16)
    out = (x.astype(F32) + matmul(attended, output_w[...])).astype(BF16)
    out_own[...] = out[:size]
    out_sibling[...] = out[size : 2 * size]
    for i in range(2):
        part = out[(2 + i) * size : (3 + i) * size]
        if len(out_opposite) == 2:
            out_opposite[i][...] = part
        else:
            out_opposite[0][i] = part


def attention(apart, *args):
    _, size, width = args[1].shape
    rows = 4 * size
    tiled = pltpu.VMEM((width // LANES, rows, LANES), F32)
    return pl.pallas_call(
        attention_kernel,
        in_specs=[WHOLE] * len(args),
        out_specs=[WHOLE] * (4 if apart else 3),
        out_shape=[array(size, width)] * 4 if apart else [array(size, width)] * 2 + [array(2, size, width)],
        scratch_shapes=[tiled] * 4 + [pltpu.VMEM((rows, width), BF16)],
        compiler_params=params(),
        cost_estimate=cost(),
    )(*args)


def finish_kernel(levels, targets, given, *refs):
    *pieces, out_ref, whole_ref, sems = refs[given:]
    chip, core = place()
    width = out_ref.shape[-1]
    lon = 3 * GROUP
    copies = []
    for n, (far, other) in enumerate(targets):
        for pair in range(levels // 2):
            rows = slice(2 * GROUP * pair, 2 * GROUP * (pair + 1))
            parts = [p[0][rows] if len(p.shape) == 3 else p[rows] for p in pieces[3 * n : 3 * n + 3]]
            whole = whole_of(*(p.astype(F32).reshape(2, GROUP, width) for p in parts))
            whole_ref[n, 2 * lon * pair : 2 * lon * (pair + 1)] = whole.reshape(2 * lon, width).astype(BF16)
        row = 2 * (1 - core if other else core) + (1 - chip if far else chip)
        copies.append(pltpu.make_async_copy(whole_ref.at[n], out_ref.at[row], sems.at[n]))
        copies[-1].start()
    for copy in copies:
        copy.wait()


def finish(levels, targets, shape, given, pieces, flops=1):
    count = len(targets)
    return pl.pallas_call(
        functools.partial(finish_kernel, levels, targets, len(given)),
        in_specs=[OUTSIDE] * len(given) + [WHOLE] * len(pieces),
        out_specs=OUTSIDE,
        out_shape=array(*shape),
        input_output_aliases={0: 0} if given else {},
        scratch_shapes=[pltpu.VMEM((count, *shape[1:]), BF16), pltpu.SemaphoreType.DMA((count,))],
        compiler_params=params(),
        cost_estimate=cost(flops),
    )(*given, *pieces)


def after(x, *others):
    return lax.optimization_barrier((x, *others))[0]


def per_device(
    nodes, level_mask, source_weight, target_weight, direction_bias, node_weight, query_key, value_weight, output_weight
):
    lat, lon, levels, width = nodes.shape
    rows = levels * lon
    opposite = [(i, i ^ 2) for i in range(4)]
    sibling = [(i, i ^ 1) for i in range(4)]
    diagonal = [(i, i ^ 3) for i in range(4)]
    ring = lax.axis_size("sector")
    up = [(i, (i + 1) % ring) for i in range(ring)]
    down = [(j, i) for i, j in up]
    far_piece = lambda c: ((True, c, 0), (True, c, 1))
    own_piece = lambda c: ((False, c, 0), (False, c, 1))

    nodes = jnp.transpose(nodes, (0, 2, 1, 3)).reshape(lat, rows, width)
    nodes_b = lax.ppermute(nodes, "level", sibling)
    far, own = {}, {}
    nodes_a, target_w, node_w, bias, source_w, *rows_a = first(
        levels, nodes, source_weight, target_weight, node_weight, direction_bias
    )
    *rows_b, to_west, to_east, far[0] = second(
        levels, far_piece(0), nodes_a, target_w, node_w, bias, source_w, *rows_a, nodes_b
    )
    shared = (nodes_a, *rows_a[:4], nodes_b, *rows_b, target_w, node_w, bias)
    then = lambda x: (after(nodes_a, x), *shared[1:])
    far[1], kept = later(levels, far_piece(1), shared, (level_mask,), "mask")
    west = lax.ppermute(to_east, "sector", up)
    east = lax.ppermute(to_west, "sector", down)
    (own[0],) = later(levels, own_piece(0), then((far[1], west)))
    arrived = [lax.ppermute(far[c], "level", opposite) for c in range(2)]
    (far[2],) = later(levels, far_piece(2), then((own[0], arrived[0])), (west, east), "edges")
    arrived += [lax.ppermute(far[2], "level", opposite)]
    done, close, back, distant = {}, {}, {}, {}
    for c in range(3):
        if c == 1:
            own[1], own[2] = later(levels, own_piece(1) + own_piece(2), then(done[0]), (west, east), "edges")
        mine = after(own[c], far[2] if c == 0 else done[c - 1])
        args = (kept, mine, arrived[c], query_key, value_weight, output_weight)
        done[c], close[c], *toward = attention(c == 2, *args)
        if c < 2:
            back[c] = lax.ppermute(toward[0], "level", opposite)
        else:
            back[c] = lax.ppermute(after(toward[0], back[0]), "level", opposite)
            distant[c] = lax.ppermute(after(toward[1], back[0]), "level", diagonal)
    shape = (lat, rows, width)
    listed = lambda d: [d[c] for c in range(3)]
    out = finish(levels, ((False, False),), shape, (), listed(done), 10**10)
    late = lambda x: after(x, out, back[0])
    for c in range(2):
        distant[c] = lax.ppermute(late(back[c][1]), "level", sibling)
    close = {0: lax.ppermute(close[0], "level", sibling)} | {
        c: lax.ppermute(late(close[c]), "level", sibling) for c in (1, 2)
    }
    targets = ((True, False), (True, True), (False, True))
    out = finish(levels, targets, shape, (out,), listed(back) + listed(distant) + listed(close))
    return jnp.transpose(out.reshape(lat, levels, lon, width), (0, 2, 1, 3))


def solution(mesh):
    placed = (P(None, "sector", "level", None), P(), P(), P(), P(), P(), P(), P(), P())
    return jax.shard_map(
        per_device,
        mesh=mesh,
        in_specs=placed,
        out_specs=P(None, "sector", "level", None),
        check_vma=False,
    )
```

```python
import functools

import jax
import jax.numpy as jnp
from jax import lax
from jax.experimental import pallas as pl
from jax.experimental.pallas import tpu as pltpu
from jax.sharding import PartitionSpec as P

HEAD = 64
EPSILON = 1e-06
MASKED = -1e30
GROUP = 8
LANES = 128
HALF = GROUP // 2
F32, BF16 = jnp.float32, jnp.bfloat16
WHOLE = pl.BlockSpec(memory_space=pltpu.VMEM)
SCALARS = pl.BlockSpec(memory_space=pltpu.SMEM)
OUTSIDE = pl.BlockSpec(memory_space=pltpu.HBM)


def array(*shape, dtype=BF16):
    return jax.ShapeDtypeStruct(shape, dtype)


def params(mib=24):
    return pltpu.CompilerParams(vmem_limit_bytes=mib << 20)


def cost(flops=1):
    return pl.CostEstimate(flops=flops, bytes_accessed=1, transcendentals=0)


def normalize(x):
    return x * lax.rsqrt(jnp.mean(x * x, axis=-1, keepdims=True) + EPSILON)


def matmul(x, weight):
    return jnp.dot(x, weight, preferred_element_type=F32)


def place():
    here = lax.axis_index("level")
    return here // 2, here % 2


def chunk_of(x, chunk):
    first, middle, last = (x[:, GROUP * i : GROUP * (i + 1)] for i in range(3))
    if chunk == 0:
        return middle
    low = lax.broadcasted_iota(jnp.int32, first.shape, 1) < HALF
    return jnp.where(low, last, first) if chunk == 1 else jnp.where(low, first, last)


def whole_of(middle, beside, outer):
    low = lax.broadcasted_iota(jnp.int32, middle.shape, 1) < HALF
    return jnp.concatenate([jnp.where(low, outer, beside), middle, jnp.where(low, beside, outer)], axis=1)


def by_chunk(x, levels):
    rows, width = x.shape
    x = x.astype(F32).reshape(levels, rows // levels, width)
    return jnp.concatenate([chunk_of(x, c).reshape(levels * GROUP, width) for c in range(3)], axis=0)


def update_pieces(pieces, levels, halves, target_w, node_w, bias_ref, edges, target_ref, sum_ref):
    chip, core = place()
    width = bias_ref.shape[-1]
    size = levels * GROUP
    side = [jnp.where(chip == (1 if far else 0), 0, 1) for far in (False, True)]
    x = [halves[h][0][core + side[far], size * c : size * (c + 1)] for far, c, h in pieces]
    target_ref[...] = matmul(jnp.concatenate(x, axis=0), target_w[...]) * 0.5
    step = LANES
    for n, (far, c, h) in enumerate(pieces):
        _, source_ref, east_ref, west_ref = halves[h][:4]
        row = core + side[far]
        lat = core + row
        north, south = jnp.maximum(row - 1, 0), jnp.minimum(row + 1, 2)
        has_north = jnp.where(lat >= 1, 1.0, 0.0)
        has_south = jnp.where(lat <= 2, 1.0, 0.0)
        if c == 2:
            west_edge = edges[0][2 * h + side[far]].astype(F32)
            east_edge = edges[1][2 * h + side[far]].astype(F32)
        for pair in range(levels // 2):
            for lane in range(0, width, step):
                cols = slice(lane, lane + step)
                rows = slice(size * c + 2 * GROUP * pair, size * c + 2 * GROUP * (pair + 1))
                at = slice(n * size + 2 * GROUP * pair, n * size + 2 * GROUP * (pair + 1))

                def put(x, place, edge):
                    place = lax.broadcasted_iota(jnp.int32, (GROUP, step), 0) == place
                    parts = [
                        jnp.where(place, edge[2 * pair + k : 2 * pair + k + 1, cols], x[GROUP * k : GROUP * (k + 1)])
                        for k in range(2)
                    ]
                    return jnp.concatenate(parts, axis=0)

                east = east_ref[side[far], rows, cols].astype(F32)
                west = west_ref[side[far], rows, cols].astype(F32)
                if c == 2:
                    west = put(west, 0, west_edge)
                    east = put(east, GROUP - 1, east_edge)
                target = target_ref[at, cols]

                def halved_silu(other, k):
                    half = target + other + bias_ref[k : k + 1, cols]
                    return half + half * jnp.tanh(half)

                total = halved_silu(east, 0) + halved_silu(west, 1)
                total = total + halved_silu(source_ref[north, rows, cols].astype(F32), 2) * has_north
                total = total + halved_silu(source_ref[south, rows, cols].astype(F32), 3) * has_south
                sum_ref[at, cols] = total.astype(BF16)
    update = matmul(sum_ref[...], node_w[...])
    out = []
    for n, (far, c, h) in enumerate(pieces):
        nodes_ref, offset = halves[h][4:]
        lon = nodes_ref.shape[1] // levels
        own = nodes_ref[offset + side[far]].astype(F32).reshape(levels, lon, width)
        own = chunk_of(own, c).reshape(size, width)
        out.append((own + update[n * size : (n + 1) * size]).astype(BF16))
    return out


def source_rows(levels, read, normed_ref, source_ref, east_ref, west_ref, raw_ref, edges, source_w):
    _, core = place()
    count, rows, width = normed_ref.shape
    size = levels * GROUP
    for i in range(count):
        normed_ref[i] = normalize(by_chunk(read(i), levels)).astype(BF16)
    normed = jnp.concatenate([normed_ref[i] for i in range(count)], axis=0)
    source = matmul(normed, source_w[...]) * 0.5
    for i in range(count):
        raw_ref[i] = source[i * rows : (i + 1) * rows]
        source_ref[i] = source[i * rows : (i + 1) * rows].astype(BF16)
    shape = (2, GROUP, LANES)
    spot = lax.broadcasted_iota(jnp.int32, shape, 1)
    for k in range(2):
        for pair in range(levels // 2):
            for lane in range(0, width, LANES):
                cols = slice(lane, lane + LANES)
                at = [slice(size * c + 2 * GROUP * pair, size * c + 2 * GROUP * (pair + 1)) for c in range(3)]
                x = [raw_ref[core + k, at[c], cols].reshape(shape) for c in range(3)]
                up = [pltpu.roll(y, GROUP - 1, 1) for y in x]
                down = [pltpu.roll(y, 1, 1) for y in x]
                last, half = spot == GROUP - 1, spot == HALF - 1
                east = [
                    jnp.where(last, up[1], up[0]),
                    jnp.where(half, up[2], jnp.where(last, up[0], up[1])),
                    jnp.where(half, up[1], up[2]),
                ]
                first, half = spot == 0, spot == HALF
                west = [
                    jnp.where(first, down[1], down[0]),
                    jnp.where(half, down[2], jnp.where(first, down[0], down[1])),
                    jnp.where(half, down[1], down[2]),
                ]
                for c in range(3):
                    east_ref[k, at[c], cols] = east[c].reshape(2 * GROUP, LANES).astype(BF16)
                    west_ref[k, at[c], cols] = west[c].reshape(2 * GROUP, LANES).astype(BF16)
        for level in range(levels):
            at = 2 * size + level * GROUP
            edges[0][k, level : level + 1] = raw_ref[core + k, at : at + 1]
            edges[1][k, level : level + 1] = raw_ref[core + k, at + GROUP - 1 : at + GROUP]


def first_kernel(
    levels, nodes_in, source_in, target_in, node_in, bias_in,
    nodes_ref, target_w, node_w, bias_ref, source_w, normed_ref, source_ref, east_ref, west_ref, begin_ref, end_ref,
    raw_ref, sems,
):
    count = nodes_ref.shape[0]
    _, core = place()
    pairs = [(nodes_in.at[core + i], nodes_ref.at[i]) for i in range(count)]
    pairs += [(source_in, source_w), (target_in, target_w), (node_in, node_w), (bias_in, bias_ref)]
    copies = [pltpu.make_async_copy(*pair, sems.at[i]) for i, pair in enumerate(pairs)]
    for copy in copies:
        copy.start()
    for copy in copies[: count + 1]:
        copy.wait()
    source_rows(
        levels, lambda i: nodes_ref[i], normed_ref, source_ref, east_ref, west_ref, raw_ref, (begin_ref, end_ref), source_w
    )
    for copy in copies[count + 1 :]:
        copy.wait()
    bias_ref[...] = bias_ref[...] * 0.5


def outside(*arrays):
    return [pltpu.with_memory_space_constraint(x, pltpu.HBM) for x in arrays]


def first(levels, nodes, source_w, target_w, node_w, bias):
    lat, rows, width = nodes.shape
    three, two, square = array(3, rows, width), array(2, rows, width), array(width, width)
    edge = array(2, levels, width, dtype=F32)
    return pl.pallas_call(
        functools.partial(first_kernel, levels),
        in_specs=[OUTSIDE] * 5,
        out_specs=[WHOLE] * 11,
        out_shape=[three, square, square, array(*bias.shape, dtype=F32), square, three, three, two, two, edge, edge],
        scratch_shapes=[pltpu.VMEM((3, rows, width), F32), pltpu.SemaphoreType.DMA((7,))],
        compiler_params=params(),
        cost_estimate=cost(),
    )(*outside(nodes, source_w, target_w, node_w, bias))


def second_kernel(
    pieces, levels, nodes_a, target_w, node_w, bias_ref, source_w, normed_a, source_a, east_a, west_a, begin_a, end_a, nodes_b,
    normed_ref, source_ref, east_ref, west_ref, to_west_ref, to_east_ref, far_ref,
    raw_ref, begin_ref, end_ref, target_ref, sum_ref,
):
    _, core = place()
    source_rows(
        levels, lambda i: nodes_b[core + i], normed_ref, source_ref, east_ref, west_ref, raw_ref, (begin_ref, end_ref), source_w
    )
    for k in range(2):
        to_west_ref[k], to_west_ref[2 + k] = begin_a[k].astype(BF16), begin_ref[k].astype(BF16)
        to_east_ref[k], to_east_ref[2 + k] = end_a[k].astype(BF16), end_ref[k].astype(BF16)
    halves = (
        (normed_a, source_a, east_a, west_a, nodes_a, core),
        (normed_ref, source_ref, east_ref, west_ref, nodes_b, 2 * core),
    )
    out = update_pieces(pieces, levels, halves, target_w, node_w, bias_ref, None, target_ref, sum_ref)
    far_ref[0], far_ref[1] = out


def second(levels, pieces, *args):
    rows, width = args[0].shape[1:]
    three, two, edge = array(3, rows, width), array(2, rows, width), array(4, levels, width)
    size = levels * GROUP
    count = len(pieces) * size
    return pl.pallas_call(
        functools.partial(second_kernel, pieces, levels),
        in_specs=[WHOLE] * len(args),
        out_specs=[WHOLE] * 7,
        out_shape=[three, three, two, two, edge, edge, array(2, size, width)],
        scratch_shapes=[pltpu.VMEM((3, rows, width), F32)]
        + [pltpu.VMEM((2, levels, width), F32)] * 2
        + [pltpu.VMEM((count, width), F32), pltpu.VMEM((count, width), BF16)],
        compiler_params=params(),
        cost_estimate=cost(),
    )(*args)


def later_kernel(pieces, levels, has, *refs):
    nodes_a, normed_a, source_a, east_a, west_a, nodes_b, normed_b, source_b, east_b, west_b = refs[:10]
    target_w, node_w, bias_ref = refs[10:13]
    refs = refs[13:]
    _, core = place()
    edges = None
    if has == "edges":
        edges, refs = refs[:2], refs[2:]
    *outs, target_ref, sum_ref = refs
    if has == "mask":
        mask_ref, *outs, kept_ref = outs
        here = lax.axis_index("level")
        for q in range(4):
            for level in range(levels):
                kept = jnp.where(mask_ref[(here ^ q) * levels + level] > 0, 0.0, MASKED).astype(F32)
                kept_ref[q * levels + level : q * levels + level + 1] = jnp.full((1, LANES), kept)
    halves = (
        (normed_a, source_a, east_a, west_a, nodes_a, core),
        (normed_b, source_b, east_b, west_b, nodes_b, 2 * core),
    )
    out = update_pieces(pieces, levels, halves, target_w, node_w, bias_ref, edges, target_ref, sum_ref)
    for i, ref in enumerate(outs):
        ref[0], ref[1] = out[2 * i : 2 * i + 2]


def later(levels, pieces, shared, more=(), has=None):
    width = shared[0].shape[-1]
    size = levels * GROUP
    count = len(pieces) * size
    args = (*shared, *more)
    specs = [WHOLE] * len(args)
    shapes = [array(2, size, width)] * (len(pieces) // 2)
    if has == "mask":
        specs[-1] = SCALARS
        shapes += [array(4 * levels, LANES, dtype=F32)]
    return pl.pallas_call(
        functools.partial(later_kernel, pieces, levels, has),
        in_specs=specs,
        out_specs=[WHOLE] * len(shapes),
        out_shape=shapes,
        scratch_shapes=[pltpu.VMEM((count, width), F32), pltpu.VMEM((count, width), BF16)],
        compiler_params=params(),
        cost_estimate=cost(),
    )(*args)


def attention_kernel(
    kept_ref, own_ref, opposite_ref, query_key, value_w, output_w,
    out_own, out_sibling, *refs,
):
    *out_opposite, q_ref, k_ref, v_ref, att_ref, weight_ref = refs
    _, size, width = own_ref.shape
    levels = 4 * size // GROUP
    tiles = width // LANES
    x = jnp.concatenate([own_ref[0], own_ref[1], opposite_ref[0], opposite_ref[1]], axis=0)
    normed = normalize(x.astype(F32)).astype(BF16)

    def spread(ref, y):
        for t in range(tiles):
            ref[t] = y[:, LANES * t : LANES * (t + 1)]

    spread(q_ref, matmul(normed, query_key[0]) * HEAD**-0.5)
    spread(k_ref, matmul(normed, query_key[1]))
    spread(v_ref, matmul(normed, value_w[...]))
    low = lax.broadcasted_iota(jnp.int32, (levels, LANES), 1) < HEAD
    pad = jnp.zeros((LANES - 2 * levels, LANES), BF16)
    kept = kept_ref[...]
    for column in range(GROUP):
        rows = pl.ds(column, levels, stride=GROUP)
        for t in range(tiles):
            query, key = q_ref[t, rows, :].astype(BF16), k_ref[t, rows, :].astype(BF16)
            zero = jnp.zeros_like(query)
            both = jnp.concatenate([jnp.where(low, query, zero), jnp.where(low, zero, query), pad], axis=0)
            scores = lax.dot_general(key, both, (((1,), (1,)), ((), ())), preferred_element_type=F32)
            scores = scores + kept
            weights = jnp.exp(scores - jnp.max(scores, axis=0, keepdims=True))
            weights = weights * (1.0 / jnp.sum(weights, axis=0, keepdims=True))
            weight_ref[levels * column : levels * (column + 1), LANES * t : LANES * (t + 1)] = weights.astype(BF16)
    for column in range(GROUP):
        rows = pl.ds(column, levels, stride=GROUP)
        for t in range(tiles):
            weights = weight_ref[levels * column : levels * (column + 1), LANES * t : LANES * (t + 1)]
            value = v_ref[t, rows, :].astype(BF16)
            mixed = lax.dot_general(weights, value, (((0,), (0,)), ((), ())), preferred_element_type=F32)
            att_ref[t, rows, :] = jnp.where(low, mixed[:levels], mixed[levels : 2 * levels])
    attended = jnp.concatenate([att_ref[t] for t in range(tiles)], axis=1).astype(BF16)
    out = (x.astype(F32) + matmul(attended, output_w[...])).astype(BF16)
    out_own[...] = out[:size]
    out_sibling[...] = out[size : 2 * size]
    for i in range(2):
        part = out[(2 + i) * size : (3 + i) * size]
        if len(out_opposite) == 2:
            out_opposite[i][...] = part
        else:
            out_opposite[0][i] = part


def attention(apart, *args):
    _, size, width = args[1].shape
    rows = 4 * size
    tiled = pltpu.VMEM((width // LANES, rows, LANES), F32)
    return pl.pallas_call(
        attention_kernel,
        in_specs=[WHOLE] * len(args),
        out_specs=[WHOLE] * (4 if apart else 3),
        out_shape=[array(size, width)] * 4 if apart else [array(size, width)] * 2 + [array(2, size, width)],
        scratch_shapes=[tiled] * 4 + [pltpu.VMEM((rows, width), BF16)],
        compiler_params=params(),
        cost_estimate=cost(),
    )(*args)


def finish_kernel(levels, targets, given, *refs):
    *pieces, out_ref, whole_ref, sems = refs[given:]
    chip, core = place()
    width = out_ref.shape[-1]
    lon = 3 * GROUP
    copies = []
    for n, (far, other) in enumerate(targets):
        for pair in range(levels // 2):
            rows = slice(2 * GROUP * pair, 2 * GROUP * (pair + 1))
            parts = [p[0][rows] if len(p.shape) == 3 else p[rows] for p in pieces[3 * n : 3 * n + 3]]
            whole = whole_of(*(p.astype(F32).reshape(2, GROUP, width) for p in parts))
            whole_ref[n, 2 * lon * pair : 2 * lon * (pair + 1)] = whole.reshape(2 * lon, width).astype(BF16)
        row = 2 * (1 - core if other else core) + (1 - chip if far else chip)
        copies.append(pltpu.make_async_copy(whole_ref.at[n], out_ref.at[row], sems.at[n]))
        copies[-1].start()
    for copy in copies:
        copy.wait()


def finish(levels, targets, shape, given, pieces, flops=1):
    count = len(targets)
    return pl.pallas_call(
        functools.partial(finish_kernel, levels, targets, len(given)),
        in_specs=[OUTSIDE] * len(given) + [WHOLE] * len(pieces),
        out_specs=OUTSIDE,
        out_shape=array(*shape),
        input_output_aliases={0: 0} if given else {},
        scratch_shapes=[pltpu.VMEM((count, *shape[1:]), BF16), pltpu.SemaphoreType.DMA((count,))],
        compiler_params=params(),
        cost_estimate=cost(flops),
    )(*given, *pieces)


def after(x, *others):
    return lax.optimization_barrier((x, *others))[0]


def per_device(
    nodes, level_mask, source_weight, target_weight, direction_bias, node_weight, query_key, value_weight, output_weight
):
    lat, lon, levels, width = nodes.shape
    rows = levels * lon
    opposite = [(i, i ^ 2) for i in range(4)]
    sibling = [(i, i ^ 1) for i in range(4)]
    diagonal = [(i, i ^ 3) for i in range(4)]
    ring = lax.axis_size("sector")
    up = [(i, (i + 1) % ring) for i in range(ring)]
    down = [(j, i) for i, j in up]
    far_piece = lambda c: ((True, c, 0), (True, c, 1))
    own_piece = lambda c: ((False, c, 0), (False, c, 1))

    nodes = jnp.transpose(nodes, (0, 2, 1, 3)).reshape(lat, rows, width)
    nodes_b = lax.ppermute(nodes, "level", sibling)
    far, own = {}, {}
    nodes_a, target_w, node_w, bias, source_w, *rows_a = first(
        levels, nodes, source_weight, target_weight, node_weight, direction_bias
    )
    *rows_b, to_west, to_east, far[0] = second(
        levels, far_piece(0), nodes_a, target_w, node_w, bias, source_w, *rows_a, nodes_b
    )
    shared = (nodes_a, *rows_a[:4], nodes_b, *rows_b, target_w, node_w, bias)
    then = lambda x: (after(nodes_a, x), *shared[1:])
    (far[1],) = later(levels, far_piece(1), shared)
    west = lax.ppermute(to_east, "sector", up)
    east = lax.ppermute(to_west, "sector", down)
    own[0], kept = later(levels, own_piece(0), then((far[1], west)), (level_mask,), "mask")
    arrived = [lax.ppermute(far[c], "level", opposite) for c in range(2)]
    (far[2],) = later(levels, far_piece(2), then((own[0], arrived[0])), (west, east), "edges")
    arrived += [lax.ppermute(far[2], "level", opposite)]
    done, close, back, distant = {}, {}, {}, {}
    for c in range(3):
        if c == 1:
            own[1], own[2] = later(levels, own_piece(1) + own_piece(2), then(done[0]), (west, east), "edges")
        mine = after(own[c], far[2] if c == 0 else done[c - 1])
        args = (kept, mine, arrived[c], query_key, value_weight, output_weight)
        done[c], close[c], *toward = attention(c == 2, *args)
        if c < 2:
            back[c] = lax.ppermute(toward[0], "level", opposite)
        else:
            back[c] = lax.ppermute(after(toward[0], back[0]), "level", opposite)
            distant[c] = lax.ppermute(after(toward[1], back[0]), "level", diagonal)
    shape = (lat, rows, width)
    listed = lambda d: [d[c] for c in range(3)]
    out = finish(levels, ((False, False),), shape, (), listed(done), 10**10)
    late = lambda x: after(x, out, back[0])
    for c in range(2):
        distant[c] = lax.ppermute(late(back[c][1]), "level", sibling)
    close = {0: lax.ppermute(close[0], "level", sibling)} | {
        c: lax.ppermute(late(close[c]), "level", sibling) for c in (1, 2)
    }
    out = finish(levels, ((False, True),), shape, (out,), listed(close))
    out = finish(levels, ((True, False), (True, True)), shape, (out,), listed(back) + listed(distant))
    return jnp.transpose(out.reshape(lat, levels, lon, width), (0, 2, 1, 3))


def solution(mesh):
    placed = (P(None, "sector", "level", None), P(), P(), P(), P(), P(), P(), P(), P())
    return jax.shard_map(
        per_device,
        mesh=mesh,
        in_specs=placed,
        out_specs=P(None, "sector", "level", None),
        check_vma=False,
    )
```
